256 devices in a mesh: band: 32 (over x, z), chan: 8 (over y, core).
Axes of the slice: x: 4, y: 4, z: 8, core: 2. Of those that a mesh axis runs over, the one named last changes fastest.
Arguments:
- node_values: bfloat16 [1, 224, 131072], P(None, 'chan', 'band'), may hold values from -6 to 6
- block_slot: int32 [1024], P('band'), may hold values from 0 to 63, as said below
- cell_ref: int32 [3, 256, 1440], P(None, 'band'), may hold values from 0 to 8191, as said below
- cell_weight: float32 [3, 256, 1440], P(None, 'band'), may hold values from 0.2 to 1
- target_spectrum: bfloat16 [1, 224, 256, 2, 640], P(None, 'chan', 'band'), may hold values from -48 to 48
- spec_weight: float32 [640], replicated, may hold values from 0.1 to 1
Outputs:
- node_grad: bfloat16 [1, 224, 131072], P(None, 'chan', 'band')
The draws below stay inside these ranges and needn't reach their ends.
Inputs may be any that keep to these rules, and one draw needn't show every extreme that they name: `block_slot`: each node owner's 32 consecutive entries are distinct slots; slot v belongs to band owner v // 2, and a node owner fills either none or all 2 slots of a band owner. Some band owner gets 2 blocks from every node owner, and every band owner gets blocks from at least one node owner. `cell_ref`: an entry of latitude row a always names a slot e of step one that its node owner fills with a block for band owner a // 8.
All inputs are finite; a program needn't handle non-finite values.
Results may differ from the reference program's by a relative error of at most 0.0056.
Values may be sent and summed in bfloat16 or wider, within the bound.
No kernel may reach another device: no remote copies, remote signals or barrier semaphores. Data moves between devices by JAX's collectives and lax.ppermute only.
A program may use at most 128 MiB of HBM per device.

```python
import math
import jax
import jax.numpy as jnp
from jax import lax

S = 1
C = 224
LON = 1440
K = 640
J = 3
NB = 128
LAT_DEV = 8
NBLK_DEV = 32
CAP = 2
PICKS = 16
LAT = 256
NODES = 131072
N_BAND = 32


def layout_picks(key):
    noise_draw = jax.random.randint(key, (N_BAND, N_BAND), 0, 1024)
    source = jnp.arange(N_BAND, dtype=jnp.int32)[:, None]
    band_row = jnp.arange(N_BAND, dtype=jnp.int32)[None, :]
    middle = N_BAND // 2
    nearness = 1024 - jnp.abs(2 * band_row - N_BAND) * 1024 // N_BAND
    band_bias = jnp.where((band_row == source) | (band_row == middle), 4096, nearness)
    scores = (noise_draw + band_bias) * N_BAND + band_row
    best_scores, chosen = lax.top_k(scores, PICKS)
    return chosen.astype(jnp.int32)


def draw_block_slot(key, part):
    chosen = layout_picks(key)
    position = jnp.arange(NBLK_DEV, dtype=jnp.int32)
    destination = chosen[:, position // CAP]
    slot_table = destination * CAP + (position % CAP)[None, :]
    return slot_table.reshape(-1).astype(jnp.int32)


def draw_cell_ref(key, part):
    chosen = layout_picks(key)
    key = jax.random.fold_in(key, 12)
    filled = jnp.zeros((N_BAND, N_BAND), jnp.int32).at[chosen, jnp.arange(N_BAND, dtype=jnp.int32)[:, None]].set(1)
    first_key, second_key, third_key = jax.random.split(key, 3)
    shape_all = (J, LAT, LON)
    band_row = jnp.broadcast_to((jnp.arange(LAT, dtype=jnp.int32) // LAT_DEV)[None, :, None], shape_all)
    candidate = jax.random.randint(first_key, shape_all, 0, N_BAND)
    source = jnp.where(filled[band_row, candidate] == 1, candidate, band_row)
    slot_index = jax.random.randint(second_key, shape_all, 0, CAP)
    offset = jax.random.randint(third_key, shape_all, 0, NB)
    return ((source * CAP + slot_index) * NB + offset).astype(jnp.int32)


def draw_target_spectrum(key, part):
    key = jax.random.fold_in(key, 13)
    first_key = jax.random.fold_in(key, 0)
    shape_all = (S, C, LAT, 2, K)
    channel = jnp.arange(C, dtype=jnp.float32)[None, :, None, None, None]
    wavenumber = jnp.arange(K, dtype=jnp.float32)[None, None, None, None, :]
    row_place = jnp.arange(LAT, dtype=jnp.float32)[None, None, :, None, None] / LAT
    decay_factor = 1.0 / (1.0 + 2.0 * wavenumber / K)
    channel_scale = 1.0 + 2.0 * channel / C
    base_draw = jnp.clip(jax.random.normal(first_key, shape_all, jnp.float32), -2.5, 2.5) * (1.0 + 2.0 * row_place)
    return (base_draw * decay_factor * channel_scale).astype(jnp.bfloat16)


def block_scale(own_key, extent, pieces, least, high):
    gain = 1.0
    for dim, parts in pieces:
        steps = jax.random.uniform(jax.random.fold_in(jax.random.fold_in(own_key, 6), dim), (parts,), jnp.float32, least / len(pieces), high / len(pieces))
        gain = gain * jnp.repeat(jnp.exp(steps), extent[dim] // parts).reshape((-1,) + (1,) * (len(extent) - 1 - dim))
    return gain


def normal_values(key, dims, deviation, reach, pieces=(), held_as=jnp.bfloat16):
    array = jax.random.normal(key, dims, jnp.float32) * deviation
    if len(pieces) > 0:
        array = block_scale(key, dims, pieces, -0.22, 0.18) * array
    return jnp.clip(array, min=-reach, max=reach).astype(held_as)


def setup_inputs(seed: int = 0) -> dict:
    streams_of = jax.random.split(jax.random.key(seed), 7)
    node_values = normal_values(streams_of[0], (S, C, NODES), 1.0, 6.0, ((1, 8), (2, 32)))
    block_slot = draw_block_slot(jax.random.fold_in(streams_of[6], 71), 0)
    cell_ref = draw_cell_ref(jax.random.fold_in(streams_of[6], 71), 0)
    cell_weight = jnp.clip(0.2 + 0.8 * jax.random.uniform(streams_of[3], (J, LAT, LON), jnp.float32) ** block_scale(streams_of[3], (J, LAT, LON), ((1, 32),), -0.2, 0.2), 0.2, 1.0)
    target_spectrum = draw_target_spectrum(jax.random.fold_in(streams_of[6], 71), 0)
    spec_weight = jnp.clip(jnp.exp(jax.random.uniform(streams_of[5], (K,), jnp.float32, math.log(0.1), math.log(1.0))), 0.1, 1.0)
    return dict(node_values=node_values, block_slot=block_slot, cell_ref=cell_ref, cell_weight=cell_weight, target_spectrum=target_spectrum, spec_weight=spec_weight)


epsilon = 1e-06

def dft_table():
    wavenumber = jnp.arange(K, dtype=jnp.int32)[:, None]
    column = jnp.arange(LON, dtype=jnp.int32)[None, :]
    phase_count = wavenumber * column % LON
    phase_angle = 2.0 * math.pi / LON * phase_count.astype(jnp.float32)
    norm_factor = 1.0 / math.sqrt(LON)
    return jnp.stack([jnp.cos(phase_angle) * norm_factor, -jnp.sin(phase_angle) * norm_factor]).astype(jnp.bfloat16)

def lat_weights(first_row, row_count, lat_total):
    row_index = first_row + jnp.arange(row_count, dtype=jnp.int32)
    latitude = (row_index.astype(jnp.float32) + 0.5) * (math.pi / lat_total) - 0.5 * math.pi
    return jnp.cos(latitude)

def power_sums(spectrum, target, lat_weight):
    predicted = spectrum.astype(jnp.float32)
    observed = target.astype(jnp.float32)
    weight = lat_weight[None, :, None, None]
    return (lax.optimization_barrier(jnp.sum(weight * predicted * predicted, axis=(1, 2))), lax.optimization_barrier(jnp.sum(weight * observed * observed, axis=(1, 2))), lax.optimization_barrier(jnp.sum(weight * predicted * observed, axis=(1, 2))))

def amplitude_grad(spectrum, target, lat_weight, pred_power, true_power, cross_sum, loss_scale):
    amp_pred = jnp.sqrt(pred_power + epsilon)
    amp_true = jnp.sqrt(true_power + epsilon)
    d_pred = loss_scale * (4.0 * amp_pred - 2.0 * amp_true - cross_sum * (1.0 / amp_true - amp_true / (amp_pred * amp_pred))) / (2.0 * amp_pred)
    d_cross = -loss_scale * (amp_pred / amp_true + amp_true / amp_pred)
    weight = lat_weight[None, :, None, None]
    result = weight * (2.0 * spectrum.astype(jnp.float32) * d_pred[:, None, None, :] + target.astype(jnp.float32) * d_cross[:, None, None, :])
    return result.astype(jnp.bfloat16)

def reference(node_values, block_slot, cell_ref, cell_weight, target_spectrum, spec_weight):
    transform = dft_table().astype(jnp.float32)
    slot_table = block_slot.reshape(N_BAND, NBLK_DEV)
    owners = jnp.arange(N_BAND, dtype=jnp.int32)[:, None]
    positions = jnp.broadcast_to(jnp.arange(NBLK_DEV, dtype=jnp.int32)[None, :], (N_BAND, NBLK_DEV))
    inverse = jnp.zeros((N_BAND, N_BAND * CAP), jnp.int32).at[owners, slot_table].set(positions)
    band_of_row = (jnp.arange(LAT, dtype=jnp.int32) // LAT_DEV)[None, :, None]
    source = cell_ref // (CAP * NB)
    slot_index = cell_ref // NB % CAP
    offset = cell_ref % NB
    member_block = inverse[source, band_of_row * CAP + slot_index]
    node_index = ((source * NBLK_DEV + member_block) * NB + offset).astype(jnp.int32)
    lat_weight = lat_weights(0, LAT, LAT)

    def one_sample(sample_pair):
        node_rows, target = sample_pair
        grid_values = jnp.zeros((C, LAT, LON), jnp.float32)
        for member in range(J):
            grid_values = grid_values + cell_weight[member][None] * node_rows[:, node_index[member]].astype(jnp.float32)
        grid_values = grid_values.astype(jnp.bfloat16)
        spectrum = jnp.einsum('cal,rkl->cark', grid_values.astype(jnp.float32), transform).astype(jnp.bfloat16)
        pred_power, true_power, cross_sum = power_sums(spectrum, target, lat_weight)
        energy = jnp.sum(spec_weight[None, :] * true_power) / (C * K * LAT) + epsilon
        loss_scale = jnp.broadcast_to(spec_weight[None, :] / energy, (C, K))
        spectrum_grad = amplitude_grad(spectrum, target, lat_weight, pred_power, true_power, cross_sum, loss_scale)
        grid_grad = jnp.einsum('cark,rkl->cal', spectrum_grad.astype(jnp.float32), transform)
        node_grad = jnp.zeros((C, N_BAND * NBLK_DEV * NB), jnp.float32)
        for member in range(J):
            node_grad = node_grad.at[:, node_index[member]].add(cell_weight[member][None] * grid_grad)
        return node_grad.astype(jnp.bfloat16)
    return lax.map(one_sample, (node_values, target_spectrum))
```

```python
import functools
import math

import jax
import jax.numpy as jnp
import numpy as np
from jax import lax
from jax.experimental import pallas as pl
from jax.experimental.pallas import tpu as pltpu
from jax.sharding import PartitionSpec as P

C = 224
LON = 1440
K = 640
J = 3
NB = 128
LAT_DEV = 8
NBLK_DEV = 32
CAP = 2

LONP = 1536
TILE = 256
LO = CAP * NB
CP = 32
ROWS = LAT_DEV * CP

epsilon = 1e-06


def dft_table():
    wavenumber = np.arange(K, dtype=np.int64)[:, None]
    column = np.arange(LON, dtype=np.int64)[None, :]
    phase_count = wavenumber * column % LON
    phase_angle = np.float32(2.0 * math.pi / LON) * phase_count.astype(np.float32)
    norm_factor = np.float32(1.0 / math.sqrt(LON))
    table = np.stack([np.cos(phase_angle) * norm_factor, -np.sin(phase_angle) * norm_factor])
    table = table.astype(jnp.bfloat16).reshape(2 * K, LON)
    return np.pad(table, ((0, 0), (0, LONP - LON)))


def lat_weights(first_row, row_count, lat_total):
    row_index = first_row + jnp.arange(row_count, dtype=jnp.int32)
    latitude = (row_index.astype(jnp.float32) + 0.5) * (math.pi / lat_total) - 0.5 * math.pi
    return jnp.cos(latitude)


def pack_kernel(slot_ref, nodes_ref, out_ref):
    out_ref[...] = jnp.zeros_like(out_ref)
    for i in range(NBLK_DEV):
        slot = slot_ref[i]
        half = pl.ds(pl.multiple_of((slot & 1) * NB, NB), NB)
        out_ref[slot >> 1, :, half] = nodes_ref[:, i * NB : (i + 1) * NB]


def unpack_kernel(slot_ref, scale_ref, blocks_ref, out_ref):
    scale = scale_ref[0]
    for i in range(NBLK_DEV):
        slot = slot_ref[i]
        half = pl.ds(pl.multiple_of((slot & 1) * NB, NB), NB)
        block = blocks_ref[slot >> 1, :, half].astype(jnp.float32) * scale
        out_ref[:, i * NB : (i + 1) * NB] = block.astype(jnp.bfloat16)


def one_hot(ref_row):
    owner = ref_row >> 8
    place = ref_row & (LO - 1)
    rows = lax.broadcasted_iota(jnp.int32, (LO, ref_row.shape[1]), 0)
    return owner, (rows == place).astype(jnp.float32).astype(jnp.bfloat16)


def forward_kernel(owners, lat_ref, buf_ref, cell_ref, weight_ref, table_ref, target_ref,
                   spec_ref, sums_ref, nodes, grid):
    chans = buf_ref.shape[1]
    nodes[...] = jnp.zeros_like(nodes)
    for o in range(owners):
        nodes[o * CP : o * CP + chans, :] = buf_ref[o]

    def row(a, _):
        for t in range(LONP // TILE):
            cols = slice(t * TILE, (t + 1) * TILE)
            total = jnp.zeros((CP, TILE), jnp.float32)
            for m in range(J):
                refs = cell_ref[m, pl.ds(a, 1), cols]
                owner, hot = one_hot(refs)
                picked = jnp.dot(nodes[...], hot, preferred_element_type=jnp.float32)
                value = jnp.zeros((CP, TILE), jnp.float32)
                for o in range(owners):
                    value = jnp.where(owner == o, picked[o * CP : (o + 1) * CP], value)
                total = total + weight_ref[m, pl.ds(a, 1), cols] * value
            grid[pl.ds(pl.multiple_of(a * CP, CP), CP), cols] = total.astype(jnp.bfloat16)
        return 0

    lax.fori_loop(0, LAT_DEV, row, 0)
    spectrum = lax.dot_general(
        grid[...], table_ref[...], (((1,), (1,)), ((), ())), preferred_element_type=jnp.float32
    )
    spec_ref[...] = spectrum.astype(jnp.bfloat16)
    pred = jnp.zeros((CP, 2 * K), jnp.float32)
    true = jnp.zeros((CP, 2 * K), jnp.float32)
    cross = jnp.zeros((CP, 2 * K), jnp.float32)
    for a in range(LAT_DEV):
        s = spec_ref[a * CP : (a + 1) * CP, :].astype(jnp.float32)
        g = target_ref[a * CP : (a + 1) * CP, :].astype(jnp.float32)
        ws = lat_ref[a] * s
        pred = pred + ws * s
        cross = cross + ws * g
        true = true + lat_ref[a] * g * g
    sums_ref[0] = pred[:, :K] + pred[:, K:]
    sums_ref[1] = true[:, :K] + true[:, K:]
    sums_ref[2] = cross[:, :K] + cross[:, K:]


def backward_kernel(owners, lat_ref, cell_ref, weight_ref, table_ref, target_ref, spec_ref,
                    sums_ref, spec_weight_ref, out_ref, grads, total, gated):
    chans = out_ref.shape[1]
    pred_power, true_power, cross_sum = sums_ref[0], sums_ref[1], sums_ref[2]
    loss_scale = spec_weight_ref[...]
    amp_pred = jnp.sqrt(pred_power + epsilon)
    amp_true = jnp.sqrt(true_power + epsilon)
    d_pred = (
        loss_scale
        * (
            4.0 * amp_pred
            - 2.0 * amp_true
            - cross_sum * (1.0 / amp_true - amp_true / (amp_pred * amp_pred))
        )
        / (2.0 * amp_pred)
    )
    d_cross = -loss_scale * (amp_pred / amp_true + amp_true / amp_pred)
    for a in range(LAT_DEV):
        rows = slice(a * CP, (a + 1) * CP)
        for r in range(2):
            cols = slice(r * K, (r + 1) * K)
            s = spec_ref[rows, cols].astype(jnp.float32)
            g = target_ref[rows, cols].astype(jnp.float32)
            grads[rows, cols] = (lat_ref[a] * (2.0 * s * d_pred + g * d_cross)).astype(jnp.bfloat16)
    grid_grad = jnp.dot(grads[...], table_ref[...], preferred_element_type=jnp.float32)
    gated_grad = grid_grad
    total[...] = jnp.zeros_like(total)
    gated[...] = gated_grad

    def row(a, _):
        for t in range(LONP // TILE):
            cols = slice(t * TILE, (t + 1) * TILE)
            value = gated[pl.ds(pl.multiple_of(a * CP, CP), CP), cols]
            for m in range(J):
                refs = cell_ref[m, pl.ds(a, 1), cols]
                owner, hot = one_hot(refs)
                part = weight_ref[m, pl.ds(a, 1), cols] * value
                spread = jnp.concatenate(
                    [jnp.where(owner == o, part, 0.0).astype(jnp.bfloat16) for o in range(owners)],
                    axis=0,
                )
                total[...] += lax.dot_general(
                    spread, hot, (((1,), (1,)), ((), ())), preferred_element_type=jnp.float32
                )
        return 0

    lax.fori_loop(0, LAT_DEV, row, 0)
    for o in range(owners):
        out_ref[o] = total[o * CP : o * CP + chans, :].astype(jnp.bfloat16)


SMEM = pl.BlockSpec(memory_space=pltpu.SMEM)
VMEM = pl.BlockSpec(memory_space=pltpu.VMEM)
PARAMS = pltpu.CompilerParams(vmem_limit_bytes=40 * 1024 * 1024)


def shards(node_values, block_slot, cell_ref, cell_weight, target_spectrum, spec_weight):
    owners = lax.axis_size("band")
    band_index = lax.axis_index("band")
    samples, chans, nodes_local = node_values.shape
    lat_total = LAT_DEV * owners
    lat_weight = lat_weights(band_index * LAT_DEV, LAT_DEV, lat_total)
    table = jnp.asarray(dft_table())

    outgoing = pl.pallas_call(
        pack_kernel,
        out_shape=jax.ShapeDtypeStruct((owners, chans, LO), jnp.bfloat16),
        in_specs=[SMEM, VMEM],
        out_specs=VMEM,
        compiler_params=PARAMS,
        name="pack",
    )(block_slot, node_values[0])
    received = lax.all_to_all(outgoing, "band", split_axis=0, concat_axis=0, tiled=True)

    pad = ((0, 0), (0, 0), (0, LONP - LON))
    refs = jnp.pad(cell_ref, pad, constant_values=-1)
    weights = jnp.pad(cell_weight, pad)
    target = jnp.pad(
        jnp.transpose(target_spectrum[0].reshape(chans, LAT_DEV, 2 * K), (1, 0, 2)),
        ((0, 0), (0, CP - chans), (0, 0)),
    ).reshape(ROWS, 2 * K)

    spectrum, sums = pl.pallas_call(
        functools.partial(forward_kernel, owners),
        out_shape=(
            jax.ShapeDtypeStruct((ROWS, 2 * K), jnp.bfloat16),
            jax.ShapeDtypeStruct((3, CP, K), jnp.float32),
        ),
        in_specs=[SMEM] + [VMEM] * 5,
        out_specs=(VMEM, VMEM),
        scratch_shapes=[
            pltpu.VMEM((owners * CP, LO), jnp.bfloat16),
            pltpu.VMEM((ROWS, LONP), jnp.bfloat16),
        ],
        compiler_params=PARAMS,
        name="forward",
    )(lat_weight, received, refs, weights, table, target)

    sums = lax.psum(sums, "band")
    energy_part = jnp.sum(sums[1, :chans] * spec_weight[None, :])
    energy = lax.psum(energy_part, "chan") / (C * K * lat_total) + epsilon

    slot_grad = pl.pallas_call(
        functools.partial(backward_kernel, owners),
        out_shape=jax.ShapeDtypeStruct((owners, chans, LO), jnp.bfloat16),
        in_specs=[SMEM] + [VMEM] * 7,
        out_specs=VMEM,
        scratch_shapes=[
            pltpu.VMEM((ROWS, 2 * K), jnp.bfloat16),
            pltpu.VMEM((owners * CP, LO), jnp.float32),
            pltpu.VMEM((ROWS, LONP), jnp.float32),
        ],
        compiler_params=PARAMS,
        name="backward",
    )(lat_weight, refs, weights, table, target, spectrum, sums, spec_weight[None, :])

    returned = lax.all_to_all(slot_grad, "band", split_axis=0, concat_axis=0, tiled=True)
    node_grad = pl.pallas_call(
        unpack_kernel,
        out_shape=jax.ShapeDtypeStruct((chans, nodes_local), jnp.bfloat16),
        in_specs=[SMEM, SMEM, VMEM],
        out_specs=VMEM,
        compiler_params=PARAMS,
        name="unpack",
    )(block_slot, (1.0 / energy).reshape(1), returned)
    return node_grad[None]


def solution(mesh):
    in_specs = (
        P(None, "chan", "band"),
        P("band"),
        P(None, "band", None),
        P(None, "band", None),
        P(None, "chan", "band", None, None),
        P(),
    )
    out_specs = P(None, "chan", "band")
    return jax.shard_map(shards, mesh=mesh, in_specs=in_specs, out_specs=out_specs, check_vma=False)
```

```python
import functools
import math

import jax
import jax.numpy as jnp
import numpy as np
from jax import lax
from jax.experimental import pallas as pl
from jax.experimental.pallas import tpu as pltpu
from jax.sharding import PartitionSpec as P

C = 224
LON = 1440
K = 640
J = 3
NB = 128
LAT_DEV = 8
NBLK_DEV = 32
CAP = 2

LONP = 1536
TILE = 256
LO = CAP * NB
CP = 32
ROWS = LAT_DEV * CP

epsilon = 1e-06


def dft_table():
    wavenumber = np.arange(K, dtype=np.int64)[:, None]
    column = np.arange(LON, dtype=np.int64)[None, :]
    phase_count = wavenumber * column % LON
    phase_angle = np.float32(2.0 * math.pi / LON) * phase_count.astype(np.float32)
    norm_factor = np.float32(1.0 / math.sqrt(LON))
    table = np.stack([np.cos(phase_angle) * norm_factor, -np.sin(phase_angle) * norm_factor])
    table = table.astype(jnp.bfloat16).reshape(2 * K, LON)
    return np.pad(table, ((0, 0), (0, LONP - LON)))


def lat_weights(first_row, row_count, lat_total):
    row_index = first_row + jnp.arange(row_count, dtype=jnp.int32)
    latitude = (row_index.astype(jnp.float32) + 0.5) * (math.pi / lat_total) - 0.5 * math.pi
    return jnp.cos(latitude)


def pack_kernel(slot_ref, nodes_ref, out_ref):
    out_ref[...] = jnp.zeros_like(out_ref)
    for i in range(NBLK_DEV):
        slot = slot_ref[i]
        half = pl.ds(pl.multiple_of((slot & 1) * NB, NB), NB)
        out_ref[slot >> 1, :, half] = nodes_ref[:, i * NB : (i + 1) * NB]


def unpack_kernel(slot_ref, blocks_ref, out_ref):
    for i in range(NBLK_DEV):
        slot = slot_ref[i]
        half = pl.ds(pl.multiple_of((slot & 1) * NB, NB), NB)
        out_ref[:, i * NB : (i + 1) * NB] = blocks_ref[slot >> 1, :, half]


def true_kernel(lat_ref, spec_weight_ref, target_ref, true_ref, energy_ref):
    true = jnp.zeros((CP, 2 * K), jnp.float32)
    for a in range(LAT_DEV):
        g = target_ref[a * CP : (a + 1) * CP, :].astype(jnp.float32)
        true = true + lat_ref[a] * g * g
    true = true[:, :K] + true[:, K:]
    true_ref[...] = true
    energy = jnp.sum(true * spec_weight_ref[...], axis=(0, 1), keepdims=True)
    energy_ref[...] = jnp.broadcast_to(energy, energy_ref.shape)


def middle_kernel(scale, parts_ref, spec_weight_ref, out_ref):
    sums = jnp.sum(parts_ref[...], axis=0)
    pred_power, true_power, cross_sum = sums[0:1], sums[1:2], sums[2:3]
    energy = sums[3:4] * scale + epsilon
    loss_scale = spec_weight_ref[...] / energy
    amp_pred = jnp.sqrt(pred_power + epsilon)
    amp_true = jnp.sqrt(true_power + epsilon)
    d_pred = (
        loss_scale
        * (
            4.0 * amp_pred
            - 2.0 * amp_true
            - cross_sum * (1.0 / amp_true - amp_true / (amp_pred * amp_pred))
        )
        / (2.0 * amp_pred)
    )
    d_cross = -loss_scale * (amp_pred / amp_true + amp_true / amp_pred)
    both = jnp.concatenate([d_pred, d_cross], axis=0)
    out_ref[...] = jnp.broadcast_to(both[None], out_ref.shape)


def one_hot(ref_row):
    owner = ref_row >> 8
    place = ref_row & (LO - 1)
    rows = lax.broadcasted_iota(jnp.int32, (LO, ref_row.shape[1]), 0)
    return owner, (rows == place).astype(jnp.float32).astype(jnp.bfloat16)


def forward_kernel(owners, lat_ref, buf_ref, cell_ref, weight_ref, table_ref, target_ref,
                   true_ref, energy_ref, spec_ref, sums_ref, nodes, grid):
    chans = buf_ref.shape[1]
    nodes[...] = jnp.zeros_like(nodes)
    for o in range(owners):
        nodes[o * CP : o * CP + chans, :] = buf_ref[o]

    def row(a, _):
        for t in range(LONP // TILE):
            cols = slice(t * TILE, (t + 1) * TILE)
            total = jnp.zeros((CP, TILE), jnp.float32)
            for m in range(J):
                refs = cell_ref[m, pl.ds(a, 1), cols]
                owner, hot = one_hot(refs)
                picked = jnp.dot(nodes[...], hot, preferred_element_type=jnp.float32)
                value = jnp.zeros((CP, TILE), jnp.float32)
                for o in range(owners):
                    value = jnp.where(owner == o, picked[o * CP : (o + 1) * CP], value)
                total = total + weight_ref[m, pl.ds(a, 1), cols] * value
            grid[pl.ds(pl.multiple_of(a * CP, CP), CP), cols] = total.astype(jnp.bfloat16)
        return 0

    lax.fori_loop(0, LAT_DEV, row, 0)
    spectrum = lax.dot_general(
        grid[...], table_ref[...], (((1,), (1,)), ((), ())), preferred_element_type=jnp.float32
    )
    spec_ref[...] = spectrum.astype(jnp.bfloat16)
    pred = jnp.zeros((CP, 2 * K), jnp.float32)
    cross = jnp.zeros((CP, 2 * K), jnp.float32)
    for a in range(LAT_DEV):
        s = spec_ref[a * CP : (a + 1) * CP, :].astype(jnp.float32)
        g = target_ref[a * CP : (a + 1) * CP, :].astype(jnp.float32)
        ws = lat_ref[a] * s
        pred = pred + ws * s
        cross = cross + ws * g
    energy = jnp.sum(energy_ref[...], axis=0)[0:1, 0:1]
    sums_ref[:, 0, :] = pred[:, :K] + pred[:, K:]
    sums_ref[:, 1, :] = true_ref[...]
    sums_ref[:, 2, :] = cross[:, :K] + cross[:, K:]
    sums_ref[:, 3, :] = jnp.broadcast_to(energy, (CP, K))


def backward_kernel(owners, lat_ref, cell_ref, weight_ref, table_ref, target_ref, spec_ref,
                    factor_ref, out_ref, grads, total, gated):
    chans = out_ref.shape[1]
    d_pred, d_cross = factor_ref[:, 0, :], factor_ref[:, 1, :]
    for a in range(LAT_DEV):
        rows = slice(a * CP, (a + 1) * CP)
        for r in range(2):
            cols = slice(r * K, (r + 1) * K)
            s = spec_ref[rows, cols].astype(jnp.float32)
            g = target_ref[rows, cols].astype(jnp.float32)
            grads[rows, cols] = (lat_ref[a] * (2.0 * s * d_pred + g * d_cross)).astype(jnp.bfloat16)
    grid_grad = jnp.dot(grads[...], table_ref[...], preferred_element_type=jnp.float32)
    total[...] = jnp.zeros_like(total)
    gated[...] = grid_grad

    def row(a, _):
        for t in range(LONP // TILE):
            cols = slice(t * TILE, (t + 1) * TILE)
            value = gated[pl.ds(pl.multiple_of(a * CP, CP), CP), cols]
            for m in range(J):
                refs = cell_ref[m, pl.ds(a, 1), cols]
                owner, hot = one_hot(refs)
                part = weight_ref[m, pl.ds(a, 1), cols] * value
                spread = jnp.concatenate(
                    [jnp.where(owner == o, part, 0.0).astype(jnp.bfloat16) for o in range(owners)],
                    axis=0,
                )
                total[...] += lax.dot_general(
                    spread, hot, (((1,), (1,)), ((), ())), preferred_element_type=jnp.float32
                )
        return 0

    lax.fori_loop(0, LAT_DEV, row, 0)
    for o in range(owners):
        out_ref[o] = total[o * CP : o * CP + chans, :].astype(jnp.bfloat16)


SMEM = pl.BlockSpec(memory_space=pltpu.SMEM)
VMEM = pl.BlockSpec(memory_space=pltpu.VMEM)
PARAMS = pltpu.CompilerParams(vmem_limit_bytes=40 * 1024 * 1024)


def exchange(blocks, axis):
    return lax.all_to_all(blocks, axis, split_axis=0, concat_axis=0, tiled=True)


def everyone(block, axis):
    count = lax.axis_size(axis)
    return exchange(jnp.broadcast_to(block[None], (count,) + block.shape), axis)


def shards(node_values, block_slot, cell_ref, cell_weight, target_spectrum, spec_weight):
    owners = lax.axis_size("band")
    band_index = lax.axis_index("band")
    samples, chans, nodes_local = node_values.shape
    lat_total = LAT_DEV * owners
    lat_weight = lat_weights(band_index * LAT_DEV, LAT_DEV, lat_total)
    table = jnp.asarray(dft_table())

    outgoing = pl.pallas_call(
        pack_kernel,
        out_shape=jax.ShapeDtypeStruct((owners, chans, LO), jnp.bfloat16),
        in_specs=[SMEM, VMEM],
        out_specs=VMEM,
        compiler_params=PARAMS,
        name="pack",
    )(block_slot, node_values[0])
    received = exchange(outgoing, "band")

    pad = ((0, 0), (0, 0), (0, LONP - LON))
    refs = jnp.pad(cell_ref, pad, constant_values=-1)
    weights = jnp.pad(cell_weight, pad)
    target = jnp.pad(
        jnp.transpose(target_spectrum[0].reshape(chans, LAT_DEV, 2 * K), (1, 0, 2)),
        ((0, 0), (0, CP - chans), (0, 0)),
    ).reshape(ROWS, 2 * K)

    true_part, energy_part = pl.pallas_call(
        true_kernel,
        out_shape=(
            jax.ShapeDtypeStruct((CP, K), jnp.float32),
            jax.ShapeDtypeStruct((8, 128), jnp.float32),
        ),
        in_specs=[SMEM, VMEM, VMEM],
        out_specs=(VMEM, VMEM),
        compiler_params=PARAMS,
        name="true_power",
    )(lat_weight, spec_weight[None, :], target)
    energies = everyone(energy_part, "chan")

    spectrum, sums = pl.pallas_call(
        functools.partial(forward_kernel, owners),
        out_shape=(
            jax.ShapeDtypeStruct((ROWS, 2 * K), jnp.bfloat16),
            jax.ShapeDtypeStruct((CP, 4, K), jnp.float32),
        ),
        in_specs=[SMEM] + [VMEM] * 7,
        out_specs=(VMEM, VMEM),
        scratch_shapes=[
            pltpu.VMEM((owners * CP, LO), jnp.bfloat16),
            pltpu.VMEM((ROWS, LONP), jnp.bfloat16),
        ],
        compiler_params=PARAMS,
        name="forward",
    )(lat_weight, received, refs, weights, table, target, true_part, energies)

    parts = exchange(sums, "band")
    factors = pl.pallas_call(
        functools.partial(middle_kernel, 1.0 / (C * K * lat_total)),
        out_shape=jax.ShapeDtypeStruct((owners, 2, K), jnp.float32),
        in_specs=[VMEM, VMEM],
        out_specs=VMEM,
        compiler_params=PARAMS,
        name="middle",
    )(parts, spec_weight[None, :])
    factors = exchange(factors, "band")

    slot_grad = pl.pallas_call(
        functools.partial(backward_kernel, owners),
        out_shape=jax.ShapeDtypeStruct((owners, chans, LO), jnp.bfloat16),
        in_specs=[SMEM] + [VMEM] * 6,
        out_specs=VMEM,
        scratch_shapes=[
            pltpu.VMEM((ROWS, 2 * K), jnp.bfloat16),
            pltpu.VMEM((owners * CP, LO), jnp.float32),
            pltpu.VMEM((ROWS, LONP), jnp.float32),
        ],
        compiler_params=PARAMS,
        name="backward",
    )(lat_weight, refs, weights, table, target, spectrum, factors)

    returned = exchange(slot_grad, "band")
    node_grad = pl.pallas_call(
        unpack_kernel,
        out_shape=jax.ShapeDtypeStruct((chans, nodes_local), jnp.bfloat16),
        in_specs=[SMEM, VMEM],
        out_specs=VMEM,
        compiler_params=PARAMS,
        name="unpack",
    )(block_slot, returned)
    return node_grad[None]


def solution(mesh):
    in_specs = (
        P(None, "chan", "band"),
        P("band"),
        P(None, "band", None),
        P(None, "band", None),
        P(None, "chan", "band", None, None),
        P(),
    )
    out_specs = P(None, "chan", "band")
    return jax.shard_map(shards, mesh=mesh, in_specs=in_specs, out_specs=out_specs, check_vma=False)
```

```python
import functools
import math

import jax
import jax.numpy as jnp
import numpy as np
from jax import lax
from jax.experimental import pallas as pl
from jax.experimental.pallas import tpu as pltpu
from jax.sharding import PartitionSpec as P

C = 224
LON = 1440
K = 640
J = 3
NB = 128
LAT_DEV = 8
NBLK_DEV = 32
CAP = 2

LONP = 1536
TILE = 256
LO = CAP * NB
CP = 32
MAIN = LON - LON % TILE
REST = LON - MAIN
CELL_ROWS = LAT_DEV + 1
CHANS = 28
HALF = 4
BODY = CHANS - HALF
PAIR = 2 * CHANS
ROWS = LAT_DEV * CP

epsilon = 1e-06


def dft_table():
    wavenumber = np.arange(K, dtype=np.int64)[:, None]
    column = np.arange(LON, dtype=np.int64)[None, :]
    phase_count = wavenumber * column % LON
    phase_angle = np.float32(2.0 * math.pi / LON) * phase_count.astype(np.float32)
    norm_factor = np.float32(1.0 / math.sqrt(LON))
    table = np.stack([np.cos(phase_angle) * norm_factor, -np.sin(phase_angle) * norm_factor])
    table = table.astype(jnp.bfloat16).reshape(2 * K, LON)
    return np.pad(table, ((0, 0), (0, LONP - LON)))


def lat_weights(first_row, row_count, lat_total):
    row_index = first_row + jnp.arange(row_count, dtype=jnp.int32)
    latitude = (row_index.astype(jnp.float32) + 0.5) * (math.pi / lat_total) - 0.5 * math.pi
    return jnp.cos(latitude)


def pack_kernel(slot_ref, nodes_ref, out_ref):
    out_ref[...] = jnp.zeros_like(out_ref)
    for i in range(NBLK_DEV):
        slot = slot_ref[i]
        half = pl.ds(pl.multiple_of((slot & 1) * NB, NB), NB)
        out_ref[slot >> 1, :, half] = nodes_ref[:, i * NB : (i + 1) * NB]


def unpack_kernel(slot_ref, blocks_ref, out_ref):
    for i in range(NBLK_DEV):
        slot = slot_ref[i]
        half = pl.ds(pl.multiple_of((slot & 1) * NB, NB), NB)
        out_ref[:, i * NB : (i + 1) * NB] = blocks_ref[slot >> 1, :, half]


def true_kernel(lat_ref, spec_weight_ref, target_ref, true_ref, energy_ref):
    true = jnp.zeros((CP, 2 * K), jnp.float32)
    for a in range(LAT_DEV):
        g = target_ref[a * CP : (a + 1) * CP, :].astype(jnp.float32)
        true = true + lat_ref[a] * g * g
    true = true[:, :K] + true[:, K:]
    true_ref[...] = true
    energy = jnp.sum(true * spec_weight_ref[...], axis=(0, 1), keepdims=True)
    energy_ref[...] = jnp.broadcast_to(energy, energy_ref.shape)


def middle_kernel(scale, parts_ref, spec_weight_ref, out_ref):
    sums = jnp.sum(parts_ref[...], axis=0)
    pred_power, true_power, cross_sum = sums[0:1], sums[1:2], sums[2:3]
    energy = sums[3:4] * scale + epsilon
    loss_scale = spec_weight_ref[...] / energy
    amp_pred = jnp.sqrt(pred_power + epsilon)
    amp_true = jnp.sqrt(true_power + epsilon)
    d_pred = (
        loss_scale
        * (
            4.0 * amp_pred
            - 2.0 * amp_true
            - cross_sum * (1.0 / amp_true - amp_true / (amp_pred * amp_pred))
        )
        / (2.0 * amp_pred)
    )
    d_cross = -loss_scale * (amp_pred / amp_true + amp_true / amp_pred)
    both = jnp.concatenate([d_pred, d_cross], axis=0)
    out_ref[...] = jnp.broadcast_to(both[None], out_ref.shape)


def one_hot(ref_row):
    owner = ref_row >> 8
    place = ref_row & (LO - 1)
    rows = lax.broadcasted_iota(jnp.int32, (LO, ref_row.shape[1]), 0)
    return owner, (rows == place).astype(jnp.float32).astype(jnp.bfloat16)


def shared_owner(owner):
    first = lax.broadcasted_iota(jnp.int32, (2 * HALF, owner.shape[1]), 0) < HALF
    wanted = jnp.where(first, 0, 1)
    return jnp.where((owner & 1) == wanted, owner >> 1, -1)


def forward_kernel(owners, lat_ref, buf_ref, cell_ref, weight_ref, table_hbm, target_ref,
                   true_ref, *refs):
    energy_refs = refs[:-8]
    spec_ref, sums_ref, staged, nodes, grid, tail, table_ref, table_sem = refs[-8:]
    table_copy = pltpu.make_async_copy(table_hbm, table_ref, table_sem)
    table_copy.start()
    for p in range(owners // 2):
        even = buf_ref[2 * p].astype(jnp.float32)
        odd = buf_ref[2 * p + 1].astype(jnp.float32)
        staged[p * PAIR : p * PAIR + BODY, :] = even[:BODY]
        shared = jnp.concatenate([even[BODY:], odd[BODY:]], axis=0)
        staged[p * PAIR + BODY : p * PAIR + BODY + 2 * HALF, :] = shared
        staged[p * PAIR + BODY + 2 * HALF : (p + 1) * PAIR, :] = odd[:BODY]
    nodes[...] = staged[...].astype(jnp.bfloat16)

    def row(a, _):
        for t in range(MAIN // TILE):
            cols = slice(t * TILE, (t + 1) * TILE)
            total = jnp.zeros((CP, TILE), jnp.float32)
            for m in range(J):
                owner, hot = one_hot(cell_ref[m, pl.ds(a, 1), cols])
                shared = shared_owner(owner)
                picked = jnp.dot(nodes[...], hot, preferred_element_type=jnp.float32)
                body = jnp.zeros((BODY, TILE), jnp.float32)
                half = jnp.zeros((2 * HALF, TILE), jnp.float32)
                for p in range(owners // 2):
                    block = picked[p * PAIR : (p + 1) * PAIR]
                    body = jnp.where(owner == 2 * p, block[:BODY], body)
                    half = jnp.where(shared == p, block[BODY : BODY + 2 * HALF], half)
                    body = jnp.where(owner == 2 * p + 1, block[BODY + 2 * HALF :], body)
                value = jnp.concatenate([body, half + pltpu.roll(half, HALF, 0)], axis=0)
                total = total + weight_ref[m, pl.ds(a, 1), cols] * value
            grid[pl.ds(pl.multiple_of(a * CP, CP), CP), cols] = total.astype(jnp.bfloat16)
        return 0

    lax.fori_loop(0, CELL_ROWS, row, 0)
    rest = grid[ROWS : ROWS + CP, :].astype(jnp.float32)
    for a in range(LAT_DEV):
        piece = rest[:, a * REST : (a + 1) * REST]
        piece = jnp.concatenate([piece, jnp.zeros((CP, TILE - REST), jnp.float32)], axis=1)
        tail[a * CP : (a + 1) * CP, :] = piece.astype(jnp.bfloat16)
    table_copy.wait()
    contract = (((1,), (1,)), ((), ()))
    spectrum = lax.dot_general(
        grid[:ROWS, :], table_ref[:, :MAIN], contract, preferred_element_type=jnp.float32
    ) + lax.dot_general(
        tail[...], table_ref[:, MAIN:], contract, preferred_element_type=jnp.float32
    )
    spec_ref[...] = spectrum.astype(jnp.bfloat16)
    pred = jnp.zeros((CP, 2 * K), jnp.float32)
    cross = jnp.zeros((CP, 2 * K), jnp.float32)
    for a in range(LAT_DEV):
        s = spec_ref[a * CP : (a + 1) * CP, :].astype(jnp.float32)
        g = target_ref[a * CP : (a + 1) * CP, :].astype(jnp.float32)
        ws = lat_ref[a] * s
        pred = pred + ws * s
        cross = cross + ws * g
    energy = energy_refs[0][0:1, 0:1]
    for energy_ref in energy_refs[1:]:
        energy = energy + energy_ref[0:1, 0:1]
    sums_ref[:, 0, :] = pred[:, :K] + pred[:, K:]
    sums_ref[:, 1, :] = true_ref[...]
    sums_ref[:, 2, :] = cross[:, :K] + cross[:, K:]
    sums_ref[:, 3, :] = jnp.broadcast_to(energy, (CP, K))


def backward_kernel(owners, lat_ref, cell_ref, weight_ref, table_ref, target_ref, spec_ref,
                    factor_ref, out_ref, grads, total, gated):
    d_pred, d_cross = factor_ref[:, 0, :], factor_ref[:, 1, :]
    for a in range(LAT_DEV):
        rows = slice(a * CP, (a + 1) * CP)
        for r in range(2):
            cols = slice(r * K, (r + 1) * K)
            s = spec_ref[rows, cols].astype(jnp.float32)
            g = target_ref[rows, cols].astype(jnp.float32)
            grads[rows, cols] = (lat_ref[a] * (2.0 * s * d_pred + g * d_cross)).astype(jnp.bfloat16)
    grid_grad = jnp.dot(grads[...], table_ref[...], preferred_element_type=jnp.float32)
    gated[:ROWS, :] = grid_grad[:, :MAIN]
    gated[ROWS:, :] = jnp.concatenate(
        [grid_grad[a * CP : (a + 1) * CP, MAIN:LON] for a in range(LAT_DEV)], axis=1
    )
    total[...] = jnp.zeros_like(total)

    def row(a, _):
        for t in range(MAIN // TILE):
            cols = slice(t * TILE, (t + 1) * TILE)
            value = gated[pl.ds(pl.multiple_of(a * CP, CP), CP), cols]
            for m in range(J):
                owner, hot = one_hot(cell_ref[m, pl.ds(a, 1), cols])
                shared = shared_owner(owner)
                part = weight_ref[m, pl.ds(a, 1), cols] * value
                body, last = part[:BODY], part[BODY:]
                first = lax.broadcasted_iota(jnp.int32, last.shape, 0) < HALF
                half = jnp.where(first, last, pltpu.roll(last, HALF, 0))
                pieces = []
                for p in range(owners // 2):
                    pieces.append(jnp.where(owner == 2 * p, body, 0.0))
                    pieces.append(jnp.where(shared == p, half, 0.0))
                    pieces.append(jnp.where(owner == 2 * p + 1, body, 0.0))
                spread = jnp.concatenate(pieces, axis=0).astype(jnp.bfloat16)
                total[...] += lax.dot_general(
                    spread, hot, (((1,), (1,)), ((), ())), preferred_element_type=jnp.float32
                )
        return 0

    lax.fori_loop(0, CELL_ROWS, row, 0)
    for p in range(owners // 2):
        block = total[p * PAIR : (p + 1) * PAIR, :]
        shared = block[BODY : BODY + 2 * HALF]
        even = jnp.concatenate([block[:BODY], shared[:HALF]], axis=0)
        odd = jnp.concatenate([block[BODY + 2 * HALF :], shared[HALF:]], axis=0)
        out_ref[2 * p] = even.astype(jnp.bfloat16)
        out_ref[2 * p + 1] = odd.astype(jnp.bfloat16)


SMEM = pl.BlockSpec(memory_space=pltpu.SMEM)
VMEM = pl.BlockSpec(memory_space=pltpu.VMEM)
PARAMS = pltpu.CompilerParams(vmem_limit_bytes=40 * 1024 * 1024)


def exchange(blocks, axis):
    return lax.all_to_all(blocks, axis, split_axis=0, concat_axis=0, tiled=True)


def everyone(block, axis):
    count = lax.axis_size(axis)
    shifts = [[(i, (i + d) % count) for i in range(count)] for d in range(1, count)]
    return [block] + [lax.ppermute(block, axis, shift) for shift in shifts]


def cell_rows(cells):
    rest = cells[:, :, MAIN:].reshape(J, 1, LAT_DEV * REST)
    return jnp.concatenate([cells[:, :, :MAIN], rest], axis=1)


def shards(node_values, block_slot, cell_ref, cell_weight, target_spectrum, spec_weight):
    owners = lax.axis_size("band")
    band_index = lax.axis_index("band")
    samples, chans, nodes_local = node_values.shape
    lat_total = LAT_DEV * owners
    lat_weight = lat_weights(band_index * LAT_DEV, LAT_DEV, lat_total)
    table = jnp.asarray(dft_table())

    outgoing = pl.pallas_call(
        pack_kernel,
        out_shape=jax.ShapeDtypeStruct((owners, chans, LO), jnp.bfloat16),
        in_specs=[SMEM, VMEM],
        out_specs=VMEM,
        compiler_params=PARAMS,
        name="pack",
    )(block_slot, node_values[0])
    outgoing, target_spectrum = lax.optimization_barrier((outgoing, target_spectrum))
    received = exchange(outgoing, "band")

    refs = cell_rows(cell_ref)
    weights = cell_rows(cell_weight)
    target = jnp.pad(
        jnp.transpose(target_spectrum[0].reshape(chans, LAT_DEV, 2 * K), (1, 0, 2)),
        ((0, 0), (0, CP - chans), (0, 0)),
    ).reshape(ROWS, 2 * K)

    true_part, energy_part = pl.pallas_call(
        true_kernel,
        out_shape=(
            jax.ShapeDtypeStruct((CP, K), jnp.float32),
            jax.ShapeDtypeStruct((8, 128), jnp.float32),
        ),
        in_specs=[SMEM, VMEM, VMEM],
        out_specs=(VMEM, VMEM),
        compiler_params=PARAMS,
        name="true_power",
    )(lat_weight, spec_weight[None, :], target)
    energies = everyone(energy_part, "chan")

    spectrum, sums = pl.pallas_call(
        functools.partial(forward_kernel, owners),
        out_shape=(
            jax.ShapeDtypeStruct((ROWS, 2 * K), jnp.bfloat16),
            jax.ShapeDtypeStruct((CP, 4, K), jnp.float32),
        ),
        in_specs=[SMEM] + [VMEM] * 3 + [pl.BlockSpec(memory_space=pl.ANY)]
        + [VMEM] * (2 + len(energies)),
        out_specs=(VMEM, VMEM),
        scratch_shapes=[
            pltpu.VMEM((owners * CHANS, LO), jnp.float32),
            pltpu.VMEM((owners * CHANS, LO), jnp.bfloat16),
            pltpu.VMEM((CELL_ROWS * CP, MAIN), jnp.bfloat16),
            pltpu.VMEM((ROWS, TILE), jnp.bfloat16),
            pltpu.VMEM(table.shape, jnp.bfloat16),
            pltpu.SemaphoreType.DMA,
        ],
        compiler_params=PARAMS,
        name="forward",
    )(lat_weight, received, refs, weights, table, target, true_part, *energies)

    parts = exchange(sums, "band")
    factors = pl.pallas_call(
        functools.partial(middle_kernel, 1.0 / (C * K * lat_total)),
        out_shape=jax.ShapeDtypeStruct((owners, 2, K), jnp.float32),
        in_specs=[VMEM, VMEM],
        out_specs=VMEM,
        compiler_params=PARAMS,
        name="middle",
    )(parts, spec_weight[None, :])
    factors = exchange(factors, "band")

    slot_grad = pl.pallas_call(
        functools.partial(backward_kernel, owners),
        out_shape=jax.ShapeDtypeStruct((owners, chans, LO), jnp.bfloat16),
        in_specs=[SMEM] + [VMEM] * 6,
        out_specs=VMEM,
        scratch_shapes=[
            pltpu.VMEM((ROWS, 2 * K), jnp.bfloat16),
            pltpu.VMEM((owners * CHANS, LO), jnp.float32),
            pltpu.VMEM((CELL_ROWS * CP, MAIN), jnp.float32),
        ],
        compiler_params=PARAMS,
        name="backward",
    )(lat_weight, refs, weights, table, target, spectrum, factors)

    returned = exchange(slot_grad, "band")
    node_grad = pl.pallas_call(
        unpack_kernel,
        out_shape=jax.ShapeDtypeStruct((chans, nodes_local), jnp.bfloat16),
        in_specs=[SMEM, VMEM],
        out_specs=VMEM,
        compiler_params=PARAMS,
        name="unpack",
    )(block_slot, returned)
    return node_grad[None]


def solution(mesh):
    in_specs = (
        P(None, "chan", "band"),
        P("band"),
        P(None, "band", None),
        P(None, "band", None),
        P(None, "chan", "band", None, None),
        P(),
    )
    out_specs = P(None, "chan", "band")
    return jax.shard_map(shards, mesh=mesh, in_specs=in_specs, out_specs=out_specs, check_vma=False)
```

```python
import functools
import math

import jax
import jax.numpy as jnp
import numpy as np
from jax import lax
from jax.experimental import pallas as pl
from jax.experimental.pallas import tpu as pltpu
from jax.sharding import PartitionSpec as P

C = 224
LON = 1440
K = 640
J = 3
NB = 128
LAT_DEV = 8
NBLK_DEV = 32
CAP = 2

HALF_LON = LON // 2
HALF_PAD = 768
TILE = 256
LO = CAP * NB
CP = 32
HALF_MAIN = 640
HALF_REST = HALF_LON - HALF_MAIN
MAIN = 2 * HALF_MAIN
REST = 2 * HALF_REST
CELL_ROWS = LAT_DEV + 1
CHANS = 28
HALF = 4
BODY = CHANS - HALF
PAIR = 2 * CHANS
ROWS = LAT_DEV * CP

epsilon = 1e-06


def dft_table():
    wavenumber = np.arange(K, dtype=np.int64)[:, None]
    column = np.arange(LON, dtype=np.int64)[None, :]
    phase_count = wavenumber * column % LON
    phase_angle = np.float32(2.0 * math.pi / LON) * phase_count.astype(np.float32)
    norm_factor = np.float32(1.0 / math.sqrt(LON))
    table = np.stack([np.cos(phase_angle) * norm_factor, -np.sin(phase_angle) * norm_factor])
    table = table.astype(jnp.bfloat16).reshape(2 * K, LON)[:, :HALF_LON]
    return np.pad(table, ((0, 0), (0, HALF_PAD - HALF_LON)))


def half_sign():
    wavenumber = lax.broadcasted_iota(jnp.int32, (1, 2 * K), 1)
    return jnp.where((wavenumber & 1) == 0, 1.0, -1.0)


def lat_weights(first_row, row_count, lat_total):
    row_index = first_row + jnp.arange(row_count, dtype=jnp.int32)
    latitude = (row_index.astype(jnp.float32) + 0.5) * (math.pi / lat_total) - 0.5 * math.pi
    return jnp.cos(latitude)


def pack_kernel(slot_ref, nodes_ref, out_ref):
    out_ref[...] = jnp.zeros_like(out_ref)
    for i in range(NBLK_DEV):
        slot = slot_ref[i]
        half = pl.ds(pl.multiple_of((slot & 1) * NB, NB), NB)
        out_ref[slot >> 1, :, half] = nodes_ref[:, i * NB : (i + 1) * NB]


def unpack_kernel(slot_ref, blocks_ref, out_ref):
    for i in range(NBLK_DEV):
        slot = slot_ref[i]
        half = pl.ds(pl.multiple_of((slot & 1) * NB, NB), NB)
        out_ref[:, i * NB : (i + 1) * NB] = blocks_ref[slot >> 1, :, half]


def true_kernel(lat_ref, spec_weight_ref, target_ref, true_ref, energy_ref):
    true = jnp.zeros((CP, 2 * K), jnp.float32)
    for a in range(LAT_DEV):
        g = target_ref[a * CP : (a + 1) * CP, :].astype(jnp.float32)
        true = true + lat_ref[a] * g * g
    true = true[:, :K] + true[:, K:]
    true_ref[...] = true
    energy = jnp.sum(true * spec_weight_ref[...], axis=(0, 1), keepdims=True)
    energy_ref[...] = jnp.broadcast_to(energy, energy_ref.shape)


def middle_kernel(scale, parts_ref, spec_weight_ref, out_ref):
    sums = jnp.sum(parts_ref[...], axis=0)
    pred_power, true_power, cross_sum = sums[:, :K], sums[:, K : 2 * K], sums[:, 2 * K : 3 * K]
    energy = sums[:, 3 * K : 3 * K + 1] * scale + epsilon
    loss_scale = spec_weight_ref[...] / energy
    amp_pred = jnp.sqrt(pred_power + epsilon)
    amp_true = jnp.sqrt(true_power + epsilon)
    d_pred = (
        loss_scale
        * (
            4.0 * amp_pred
            - 2.0 * amp_true
            - cross_sum * (1.0 / amp_true - amp_true / (amp_pred * amp_pred))
        )
        / (2.0 * amp_pred)
    )
    d_cross = -loss_scale * (amp_pred / amp_true + amp_true / amp_pred)
    both = jnp.concatenate([d_pred, d_cross], axis=1)
    out_ref[...] = jnp.broadcast_to(both[None], out_ref.shape)


def one_hot(ref_row):
    owner = ref_row >> 8
    place = ref_row & (LO - 1)
    rows = lax.broadcasted_iota(jnp.int32, (LO, ref_row.shape[1]), 0)
    return owner, (rows == place).astype(jnp.float32).astype(jnp.bfloat16)


def shared_owner(owner):
    first = lax.broadcasted_iota(jnp.int32, (2 * HALF, owner.shape[1]), 0) < HALF
    wanted = jnp.where(first, 0, 1)
    return jnp.where((owner & 1) == wanted, owner >> 1, -1)


def gather_kernel(owners, buf_ref, cell_ref, weight_ref, *refs):
    energy_refs = refs[:-5]
    grid_ref, energy_ref, staged, nodes, grid = refs[-5:]
    energy_ref[...] = sum((ref[...] for ref in energy_refs[1:]), energy_refs[0][...])
    for p in range(owners // 2):
        even = buf_ref[2 * p].astype(jnp.float32)
        odd = buf_ref[2 * p + 1].astype(jnp.float32)
        staged[p * PAIR : p * PAIR + BODY, :] = even[:BODY]
        shared = jnp.concatenate([even[BODY:], odd[BODY:]], axis=0)
        staged[p * PAIR + BODY : p * PAIR + BODY + 2 * HALF, :] = shared
        staged[p * PAIR + BODY + 2 * HALF : (p + 1) * PAIR, :] = odd[:BODY]
    nodes[...] = staged[...].astype(jnp.bfloat16)

    def row(a, _):
        for t in range(MAIN // TILE):
            cols = slice(t * TILE, (t + 1) * TILE)
            total = jnp.zeros((CP, TILE), jnp.float32)
            for m in range(J):
                owner, hot = one_hot(cell_ref[m, pl.ds(a, 1), cols])
                shared = shared_owner(owner)
                picked = jnp.dot(nodes[...], hot, preferred_element_type=jnp.float32)
                body = jnp.zeros((BODY, TILE), jnp.float32)
                half = jnp.zeros((2 * HALF, TILE), jnp.float32)
                for p in range(owners // 2):
                    block = picked[p * PAIR : (p + 1) * PAIR]
                    body = jnp.where(owner == 2 * p, block[:BODY], body)
                    half = jnp.where(shared == p, block[BODY : BODY + 2 * HALF], half)
                    body = jnp.where(owner == 2 * p + 1, block[BODY + 2 * HALF :], body)
                value = jnp.concatenate([body, half + pltpu.roll(half, HALF, 0)], axis=0)
                total = total + weight_ref[m, pl.ds(a, 1), cols] * value
            grid[pl.ds(pl.multiple_of(a * CP, CP), CP), cols] = total.astype(jnp.bfloat16)
        return 0

    lax.fori_loop(0, CELL_ROWS, row, 0)
    rest = grid[ROWS : ROWS + CP, :].astype(jnp.float32)
    zeros = jnp.zeros((CP, HALF_PAD - HALF_LON), jnp.float32)
    for a in range(LAT_DEV):
        for h in range(2):
            at = a * REST + h * HALF_REST
            piece = jnp.concatenate([rest[:, at : at + HALF_REST], zeros], axis=1)
            rows = slice(h * ROWS + a * CP, h * ROWS + (a + 1) * CP)
            grid_ref[rows, HALF_MAIN:] = piece.astype(jnp.bfloat16)
    for h in range(2):
        columns = slice(h * HALF_MAIN, (h + 1) * HALF_MAIN)
        grid_ref[h * ROWS : (h + 1) * ROWS, :HALF_MAIN] = grid[:ROWS, columns]


def spectrum_kernel(lat_ref, grid_ref, table_ref, target_ref, true_ref, energy_ref, spec_ref,
                    sums_ref):
    halves = lax.dot_general(
        grid_ref[...], table_ref[...], (((1,), (1,)), ((), ())),
        preferred_element_type=jnp.float32,
    )
    spectrum = halves[:ROWS] + half_sign() * halves[ROWS:]
    spec_ref[...] = spectrum.astype(jnp.bfloat16)
    pred = jnp.zeros((CP, 2 * K), jnp.float32)
    cross = jnp.zeros((CP, 2 * K), jnp.float32)
    for a in range(LAT_DEV):
        s = spec_ref[a * CP : (a + 1) * CP, :].astype(jnp.float32)
        g = target_ref[a * CP : (a + 1) * CP, :].astype(jnp.float32)
        ws = lat_ref[a] * s
        pred = pred + ws * s
        cross = cross + ws * g
    sums_ref[:, 0, :K] = pred[:, :K] + pred[:, K:]
    sums_ref[:, 0, K : 2 * K] = true_ref[...]
    sums_ref[:, 0, 2 * K : 3 * K] = cross[:, :K] + cross[:, K:]
    sums_ref[:, 0, 3 * K :] = jnp.broadcast_to(energy_ref[0:1, :], (CP, NB))


def backward_kernel(owners, lat_ref, cell_ref, weight_ref, table_ref, target_ref, spec_ref,
                    factor_ref, out_ref, grads, total, gated):
    d_pred, d_cross = factor_ref[:, 0, :K], factor_ref[:, 0, K:]
    sign = half_sign()[:, :K]
    for a in range(LAT_DEV):
        rows = slice(a * CP, (a + 1) * CP)
        for r in range(2):
            cols = slice(r * K, (r + 1) * K)
            s = spec_ref[rows, cols].astype(jnp.float32)
            g = target_ref[rows, cols].astype(jnp.float32)
            grad = lat_ref[a] * (2.0 * s * d_pred + g * d_cross)
            grads[rows, cols] = grad.astype(jnp.bfloat16)
            flipped = slice(ROWS + a * CP, ROWS + (a + 1) * CP)
            grads[flipped, cols] = (grad * sign).astype(jnp.bfloat16)
    grid_grad = jnp.dot(grads[...], table_ref[...], preferred_element_type=jnp.float32)
    rest = []
    for h in range(2):
        columns = slice(h * HALF_MAIN, (h + 1) * HALF_MAIN)
        gated[:ROWS, columns] = grid_grad[h * ROWS : (h + 1) * ROWS, :HALF_MAIN]
    for a in range(LAT_DEV):
        for h in range(2):
            rows = slice(h * ROWS + a * CP, h * ROWS + (a + 1) * CP)
            rest.append(grid_grad[rows, HALF_MAIN:HALF_LON])
    gated[ROWS:, :] = jnp.concatenate(rest, axis=1)
    total[...] = jnp.zeros_like(total)

    def row(a, _):
        for t in range(MAIN // TILE):
            cols = slice(t * TILE, (t + 1) * TILE)
            value = gated[pl.ds(pl.multiple_of(a * CP, CP), CP), cols]
            for m in range(J):
                owner, hot = one_hot(cell_ref[m, pl.ds(a, 1), cols])
                shared = shared_owner(owner)
                part = weight_ref[m, pl.ds(a, 1), cols] * value
                body, last = part[:BODY], part[BODY:]
                first = lax.broadcasted_iota(jnp.int32, last.shape, 0) < HALF
                half = jnp.where(first, last, pltpu.roll(last, HALF, 0))
                pieces = []
                for p in range(owners // 2):
                    pieces.append(jnp.where(owner == 2 * p, body, 0.0))
                    pieces.append(jnp.where(shared == p, half, 0.0))
                    pieces.append(jnp.where(owner == 2 * p + 1, body, 0.0))
                spread = jnp.concatenate(pieces, axis=0).astype(jnp.bfloat16)
                total[...] += lax.dot_general(
                    spread, hot, (((1,), (1,)), ((), ())), preferred_element_type=jnp.float32
                )
        return 0

    lax.fori_loop(0, CELL_ROWS, row, 0)
    for p in range(owners // 2):
        block = total[p * PAIR : (p + 1) * PAIR, :]
        shared = block[BODY : BODY + 2 * HALF]
        even = jnp.concatenate([block[:BODY], shared[:HALF]], axis=0)
        odd = jnp.concatenate([block[BODY + 2 * HALF :], shared[HALF:]], axis=0)
        out_ref[2 * p] = even.astype(jnp.bfloat16)
        out_ref[2 * p + 1] = odd.astype(jnp.bfloat16)


SMEM = pl.BlockSpec(memory_space=pltpu.SMEM)
VMEM = pl.BlockSpec(memory_space=pltpu.VMEM)
PARAMS = pltpu.CompilerParams(vmem_limit_bytes=24 * 1024 * 1024)


def exchange(blocks, axis):
    return lax.all_to_all(blocks, axis, split_axis=0, concat_axis=0, tiled=True)


def everyone(block, axis):
    count = lax.axis_size(axis)
    block = block + lax.ppermute(block, axis, [(i, i ^ 1) for i in range(count)])
    shifts = [[(i, (i + d) % count) for i in range(count)] for d in range(2, count, 2)]
    return [block] + [lax.ppermute(block, axis, shift) for shift in shifts]


def cell_rows(cells):
    first, second = cells[:, :, :HALF_LON], cells[:, :, HALF_LON:]
    rest = jnp.concatenate([first[:, :, HALF_MAIN:], second[:, :, HALF_MAIN:]], axis=2)
    main = jnp.concatenate([first[:, :, :HALF_MAIN], second[:, :, :HALF_MAIN]], axis=2)
    return jnp.concatenate([main, rest.reshape(J, 1, LAT_DEV * REST)], axis=1)


def shards(node_values, block_slot, cell_ref, cell_weight, target_spectrum, spec_weight):
    owners = lax.axis_size("band")
    band_index = lax.axis_index("band")
    samples, chans, nodes_local = node_values.shape
    lat_total = LAT_DEV * owners
    lat_weight = lat_weights(band_index * LAT_DEV, LAT_DEV, lat_total)
    table = jnp.asarray(dft_table())

    outgoing = pl.pallas_call(
        pack_kernel,
        out_shape=jax.ShapeDtypeStruct((owners, chans, LO), jnp.bfloat16),
        in_specs=[SMEM, VMEM],
        out_specs=VMEM,
        compiler_params=pltpu.CompilerParams(vmem_limit_bytes=60 * 1024 * 1024),
        name="pack",
    )(block_slot, node_values[0])
    outgoing, target_spectrum, cell_ref, cell_weight, spec_weight = lax.optimization_barrier(
        (outgoing, target_spectrum, cell_ref, cell_weight, spec_weight)
    )
    received = exchange(outgoing, "band")

    refs = cell_rows(cell_ref)
    weights = cell_rows(cell_weight)
    target = jnp.pad(
        jnp.transpose(target_spectrum[0].reshape(chans, LAT_DEV, 2 * K), (1, 0, 2)),
        ((0, 0), (0, CP - chans), (0, 0)),
    ).reshape(ROWS, 2 * K)

    true_part, energy_part = pl.pallas_call(
        true_kernel,
        out_shape=(
            jax.ShapeDtypeStruct((CP, K), jnp.float32),
            jax.ShapeDtypeStruct((8, 128), jnp.float32),
        ),
        in_specs=[SMEM, VMEM, VMEM],
        out_specs=(VMEM, VMEM),
        compiler_params=PARAMS,
        name="true_power",
    )(lat_weight, spec_weight[None, :], target)
    energies = everyone(energy_part, "chan")

    grid, energy = pl.pallas_call(
        functools.partial(gather_kernel, owners),
        out_shape=(
            jax.ShapeDtypeStruct((2 * ROWS, HALF_PAD), jnp.bfloat16),
            jax.ShapeDtypeStruct(energy_part.shape, jnp.float32),
        ),
        in_specs=[VMEM] * (3 + len(energies)),
        out_specs=(VMEM, VMEM),
        scratch_shapes=[
            pltpu.VMEM((owners * CHANS, LO), jnp.float32),
            pltpu.VMEM((owners * CHANS, LO), jnp.bfloat16),
            pltpu.VMEM((CELL_ROWS * CP, MAIN), jnp.bfloat16),
        ],
        compiler_params=PARAMS,
        name="gather",
    )(received, refs, weights, *energies)

    spectrum, sums = pl.pallas_call(
        spectrum_kernel,
        out_shape=(
            jax.ShapeDtypeStruct((ROWS, 2 * K), jnp.bfloat16),
            jax.ShapeDtypeStruct((CP, 1, 3 * K + NB), jnp.float32),
        ),
        in_specs=[SMEM] + [VMEM] * 5,
        out_specs=(VMEM, VMEM),
        compiler_params=PARAMS,
        name="spectrum",
    )(lat_weight, grid, table, target, true_part, energy)

    parts = exchange(sums, "band")
    factors = pl.pallas_call(
        functools.partial(middle_kernel, 1.0 / (C * K * lat_total)),
        out_shape=jax.ShapeDtypeStruct((owners, 1, 2 * K), jnp.float32),
        in_specs=[VMEM, VMEM],
        out_specs=VMEM,
        compiler_params=PARAMS,
        name="middle",
    )(parts, spec_weight[None, :])
    factors = exchange(factors, "band")

    slot_grad = pl.pallas_call(
        functools.partial(backward_kernel, owners),
        out_shape=jax.ShapeDtypeStruct((owners, chans, LO), jnp.bfloat16),
        in_specs=[SMEM] + [VMEM] * 6,
        out_specs=VMEM,
        scratch_shapes=[
            pltpu.VMEM((2 * ROWS, 2 * K), jnp.bfloat16),
            pltpu.VMEM((owners * CHANS, LO), jnp.float32),
            pltpu.VMEM((CELL_ROWS * CP, MAIN), jnp.float32),
        ],
        compiler_params=PARAMS,
        name="backward",
    )(lat_weight, refs, weights, table, target, spectrum, factors)

    returned = exchange(slot_grad, "band")
    node_grad = pl.pallas_call(
        unpack_kernel,
        out_shape=jax.ShapeDtypeStruct((chans, nodes_local), jnp.bfloat16),
        in_specs=[SMEM, VMEM],
        out_specs=VMEM,
        compiler_params=PARAMS,
        name="unpack",
    )(block_slot, returned)
    return node_grad[None]


def solution(mesh):
    in_specs = (
        P(None, "chan", "band"),
        P("band"),
        P(None, "band", None),
        P(None, "band", None),
        P(None, "chan", "band", None, None),
        P(),
    )
    out_specs = P(None, "chan", "band")
    return jax.shard_map(shards, mesh=mesh, in_specs=in_specs, out_specs=out_specs, check_vma=False)
```

```python
import functools
import math

import jax
import jax.numpy as jnp
import numpy as np
from jax import lax
from jax.experimental import pallas as pl
from jax.experimental.pallas import tpu as pltpu
from jax.sharding import PartitionSpec as P

C = 224
LON = 1440
K = 640
J = 3
NB = 128
LAT_DEV = 8
NBLK_DEV = 32
CAP = 2

HALF_LON = LON // 2
HALF_PAD = 768
TILE = 256
LO = CAP * NB
CP = 32
HALF_MAIN = 640
HALF_REST = HALF_LON - HALF_MAIN
MAIN = 2 * HALF_MAIN
REST = 2 * HALF_REST
CELL_ROWS = LAT_DEV + 1
CHANS = 28
HALF = 4
BODY = CHANS - HALF
PAIR = 2 * CHANS
ROWS = LAT_DEV * CP

epsilon = 1e-06


def dft_table():
    wavenumber = np.arange(K, dtype=np.int64)[:, None]
    column = np.arange(LON, dtype=np.int64)[None, :]
    phase_count = wavenumber * column % LON
    phase_angle = np.float32(2.0 * math.pi / LON) * phase_count.astype(np.float32)
    norm_factor = np.float32(1.0 / math.sqrt(LON))
    table = np.stack([np.cos(phase_angle) * norm_factor, -np.sin(phase_angle) * norm_factor])
    table = table.astype(jnp.bfloat16).reshape(2 * K, LON)[:, :HALF_LON]
    return np.pad(table, ((0, 0), (0, HALF_PAD - HALF_LON)))


def half_sign():
    wavenumber = lax.broadcasted_iota(jnp.int32, (1, 2 * K), 1)
    return jnp.where((wavenumber & 1) == 0, 1.0, -1.0)


def lat_weights(first_row, row_count, lat_total):
    row_index = first_row + jnp.arange(row_count, dtype=jnp.int32)
    latitude = (row_index.astype(jnp.float32) + 0.5) * (math.pi / lat_total) - 0.5 * math.pi
    return jnp.cos(latitude)


def first_rows(lanes):
    return lax.broadcasted_iota(jnp.int32, (2 * HALF, lanes), 0) < HALF


def pack_kernel(slot_ref, nodes_ref, out_ref, staged):
    staged[...] = jnp.zeros_like(staged)
    first = first_rows(NB)
    for i in range(NBLK_DEV):
        owner, slot = slot_ref[i] >> 1, slot_ref[i] & 1
        block = nodes_ref[:, i * NB : (i + 1) * NB].astype(jnp.float32)
        at = pl.multiple_of(slot * (BODY + 2 * HALF), 8)
        staged[owner, pl.ds(at, BODY), :] = block[:BODY]
        last = jnp.concatenate([block[BODY:], block[BODY:]], axis=0)
        shared = staged[owner, BODY : BODY + 2 * HALF, :]
        staged[owner, BODY : BODY + 2 * HALF, :] = jnp.where(first == (slot == 0), last, shared)
    out_ref[...] = staged[...].astype(jnp.bfloat16)


def unpack_kernel(slot_ref, blocks_ref, out_ref, staged):
    staged[...] = blocks_ref[...].astype(jnp.float32)
    for i in range(NBLK_DEV):
        owner, slot = slot_ref[i] >> 1, slot_ref[i] & 1
        at = pl.multiple_of(slot * (BODY + 2 * HALF), 8)
        body = staged[owner, pl.ds(at, BODY), :]
        shared = staged[owner, BODY : BODY + 2 * HALF, :]
        last = jnp.where(slot == 0, shared, pltpu.roll(shared, HALF, 0))[:HALF]
        block = jnp.concatenate([body, last], axis=0)
        out_ref[:, i * NB : (i + 1) * NB] = block.astype(jnp.bfloat16)


def true_kernel(lat_ref, spec_weight_ref, target_ref, true_ref, energy_ref):
    true = jnp.zeros((CP, 2 * K), jnp.float32)
    for a in range(LAT_DEV):
        g = target_ref[a * CP : (a + 1) * CP, :].astype(jnp.float32)
        true = true + lat_ref[a] * g * g
    true = true[:, :K] + true[:, K:]
    true_ref[...] = true
    energy = jnp.sum(true * spec_weight_ref[...], axis=(0, 1), keepdims=True)
    energy_ref[...] = jnp.broadcast_to(energy, energy_ref.shape)


def middle_kernel(scale, parts_ref, spec_weight_ref, out_ref):
    sums = jnp.sum(parts_ref[...], axis=0)
    pred_power, true_power, cross_sum = sums[:, :K], sums[:, K : 2 * K], sums[:, 2 * K : 3 * K]
    energy = sums[:, 3 * K : 3 * K + 1] * scale + epsilon
    loss_scale = spec_weight_ref[...] / energy
    amp_pred = jnp.sqrt(pred_power + epsilon)
    amp_true = jnp.sqrt(true_power + epsilon)
    d_pred = (
        loss_scale
        * (
            4.0 * amp_pred
            - 2.0 * amp_true
            - cross_sum * (1.0 / amp_true - amp_true / (amp_pred * amp_pred))
        )
        / (2.0 * amp_pred)
    )
    d_cross = -loss_scale * (amp_pred / amp_true + amp_true / amp_pred)
    both = jnp.concatenate([d_pred, d_cross], axis=1)
    out_ref[...] = jnp.broadcast_to(both[None], out_ref.shape)


def one_hot(ref_row):
    owner = ref_row >> 8
    place = ref_row & (LO - 1)
    rows = lax.broadcasted_iota(jnp.int32, (LO, ref_row.shape[1]), 0)
    return owner, (rows == place).astype(jnp.float32).astype(jnp.bfloat16)


def shared_owner(owner):
    first = lax.broadcasted_iota(jnp.int32, (2 * HALF, owner.shape[1]), 0) < HALF
    wanted = jnp.where(first, 0, 1)
    return jnp.where((owner & 1) == wanted, owner >> 1, -1)


def gather_kernel(owners, buf_ref, cell_ref, weight_ref, *refs):
    energy_refs = refs[:-5]
    grid_ref, energy_ref, staged, nodes, grid = refs[-5:]
    energy_ref[...] = sum((ref[...] for ref in energy_refs[1:]), energy_refs[0][...])
    first = first_rows(NB)
    for p in range(owners // 2):
        even = buf_ref[2 * p].astype(jnp.float32)
        odd = buf_ref[2 * p + 1].astype(jnp.float32)
        middle = slice(BODY, BODY + 2 * HALF)
        tail = slice(BODY + 2 * HALF, PAIR)
        at = p * PAIR
        staged[at : at + BODY, :NB], staged[at : at + BODY, NB:] = even[:BODY], even[tail]
        staged[at + BODY : at + BODY + 2 * HALF, :NB] = jnp.where(
            first, even[middle], pltpu.roll(odd[middle], HALF, 0)
        )
        staged[at + BODY : at + BODY + 2 * HALF, NB:] = jnp.where(
            first, pltpu.roll(even[middle], HALF, 0), odd[middle]
        )
        staged[at + BODY + 2 * HALF : at + PAIR, :NB] = odd[:BODY]
        staged[at + BODY + 2 * HALF : at + PAIR, NB:] = odd[tail]
    nodes[...] = staged[...].astype(jnp.bfloat16)

    def row(a, _):
        for t in range(MAIN // TILE):
            cols = slice(t * TILE, (t + 1) * TILE)
            total = jnp.zeros((CP, TILE), jnp.float32)
            for m in range(J):
                owner, hot = one_hot(cell_ref[m, pl.ds(a, 1), cols])
                shared = shared_owner(owner)
                picked = jnp.dot(nodes[...], hot, preferred_element_type=jnp.float32)
                body = jnp.zeros((BODY, TILE), jnp.float32)
                half = jnp.zeros((2 * HALF, TILE), jnp.float32)
                for p in range(owners // 2):
                    block = picked[p * PAIR : (p + 1) * PAIR]
                    body = jnp.where(owner == 2 * p, block[:BODY], body)
                    half = jnp.where(shared == p, block[BODY : BODY + 2 * HALF], half)
                    body = jnp.where(owner == 2 * p + 1, block[BODY + 2 * HALF :], body)
                value = jnp.concatenate([body, half + pltpu.roll(half, HALF, 0)], axis=0)
                total = total + weight_ref[m, pl.ds(a, 1), cols] * value
            grid[pl.ds(pl.multiple_of(a * CP, CP), CP), cols] = total.astype(jnp.bfloat16)
        return 0

    lax.fori_loop(0, CELL_ROWS, row, 0)
    rest = grid[ROWS : ROWS + CP, :].astype(jnp.float32)
    zeros = jnp.zeros((CP, HALF_PAD - HALF_LON), jnp.float32)
    for a in range(LAT_DEV):
        for h in range(2):
            at = a * REST + h * HALF_REST
            piece = jnp.concatenate([rest[:, at : at + HALF_REST], zeros], axis=1)
            rows = slice(h * ROWS + a * CP, h * ROWS + (a + 1) * CP)
            grid_ref[rows, HALF_MAIN:] = piece.astype(jnp.bfloat16)
    for h in range(2):
        columns = slice(h * HALF_MAIN, (h + 1) * HALF_MAIN)
        grid_ref[h * ROWS : (h + 1) * ROWS, :HALF_MAIN] = grid[:ROWS, columns]


def spectrum_kernel(lat_ref, grid_ref, table_ref, target_ref, true_ref, energy_ref, spec_ref,
                    sums_ref):
    halves = lax.dot_general(
        grid_ref[...], table_ref[...], (((1,), (1,)), ((), ())),
        preferred_element_type=jnp.float32,
    )
    spectrum = halves[:ROWS] + half_sign() * halves[ROWS:]
    spec_ref[...] = spectrum.astype(jnp.bfloat16)
    pred = jnp.zeros((CP, 2 * K), jnp.float32)
    cross = jnp.zeros((CP, 2 * K), jnp.float32)
    for a in range(LAT_DEV):
        s = spec_ref[a * CP : (a + 1) * CP, :].astype(jnp.float32)
        g = target_ref[a * CP : (a + 1) * CP, :].astype(jnp.float32)
        ws = lat_ref[a] * s
        pred = pred + ws * s
        cross = cross + ws * g
    sums_ref[:, 0, :K] = pred[:, :K] + pred[:, K:]
    sums_ref[:, 0, K : 2 * K] = true_ref[...]
    sums_ref[:, 0, 2 * K : 3 * K] = cross[:, :K] + cross[:, K:]
    sums_ref[:, 0, 3 * K :] = jnp.broadcast_to(energy_ref[0:1, :], (CP, NB))


def backward_kernel(owners, lat_ref, cell_ref, weight_ref, table_ref, target_ref, spec_ref,
                    factor_ref, out_ref, grads, total, gated):
    d_pred, d_cross = factor_ref[:, 0, :K], factor_ref[:, 0, K:]
    sign = half_sign()[:, :K]
    for a in range(LAT_DEV):
        rows = slice(a * CP, (a + 1) * CP)
        for r in range(2):
            cols = slice(r * K, (r + 1) * K)
            s = spec_ref[rows, cols].astype(jnp.float32)
            g = target_ref[rows, cols].astype(jnp.float32)
            grad = lat_ref[a] * (2.0 * s * d_pred + g * d_cross)
            grads[rows, cols] = grad.astype(jnp.bfloat16)
            flipped = slice(ROWS + a * CP, ROWS + (a + 1) * CP)
            grads[flipped, cols] = (grad * sign).astype(jnp.bfloat16)
    grid_grad = jnp.dot(grads[...], table_ref[...], preferred_element_type=jnp.float32)
    rest = []
    for h in range(2):
        columns = slice(h * HALF_MAIN, (h + 1) * HALF_MAIN)
        gated[:ROWS, columns] = grid_grad[h * ROWS : (h + 1) * ROWS, :HALF_MAIN]
    for a in range(LAT_DEV):
        for h in range(2):
            rows = slice(h * ROWS + a * CP, h * ROWS + (a + 1) * CP)
            rest.append(grid_grad[rows, HALF_MAIN:HALF_LON])
    gated[ROWS:, :] = jnp.concatenate(rest, axis=1)
    total[...] = jnp.zeros_like(total)

    def row(a, _):
        for t in range(MAIN // TILE):
            cols = slice(t * TILE, (t + 1) * TILE)
            value = gated[pl.ds(pl.multiple_of(a * CP, CP), CP), cols]
            for m in range(J):
                owner, hot = one_hot(cell_ref[m, pl.ds(a, 1), cols])
                shared = shared_owner(owner)
                part = weight_ref[m, pl.ds(a, 1), cols] * value
                body, last = part[:BODY], part[BODY:]
                first = lax.broadcasted_iota(jnp.int32, last.shape, 0) < HALF
                half = jnp.where(first, last, pltpu.roll(last, HALF, 0))
                pieces = []
                for p in range(owners // 2):
                    pieces.append(jnp.where(owner == 2 * p, body, 0.0))
                    pieces.append(jnp.where(shared == p, half, 0.0))
                    pieces.append(jnp.where(owner == 2 * p + 1, body, 0.0))
                spread = jnp.concatenate(pieces, axis=0).astype(jnp.bfloat16)
                total[...] += lax.dot_general(
                    spread, hot, (((1,), (1,)), ((), ())), preferred_element_type=jnp.float32
                )
        return 0

    lax.fori_loop(0, CELL_ROWS, row, 0)
    first = first_rows(NB)
    for p in range(owners // 2):
        block = total[p * PAIR : (p + 1) * PAIR, :]
        left, right = block[BODY : BODY + 2 * HALF, :NB], block[BODY : BODY + 2 * HALF, NB:]
        even = jnp.where(first, left, pltpu.roll(right, HALF, 0))
        odd = jnp.where(first, pltpu.roll(left, HALF, 0), right)
        body = block[:BODY]
        out_ref[2 * p] = jnp.concatenate([body[:, :NB], even, body[:, NB:]], axis=0).astype(
            jnp.bfloat16
        )
        body = block[BODY + 2 * HALF :]
        out_ref[2 * p + 1] = jnp.concatenate([body[:, :NB], odd, body[:, NB:]], axis=0).astype(
            jnp.bfloat16
        )


SMEM = pl.BlockSpec(memory_space=pltpu.SMEM)
VMEM = pl.BlockSpec(memory_space=pltpu.VMEM)
PARAMS = pltpu.CompilerParams(vmem_limit_bytes=24 * 1024 * 1024)


def exchange(blocks, axis):
    return lax.all_to_all(blocks, axis, split_axis=0, concat_axis=0, tiled=True)


def everyone(block, axis):
    count = lax.axis_size(axis)
    block = block + lax.ppermute(block, axis, [(i, i ^ 1) for i in range(count)])
    shifts = [[(i, (i + d) % count) for i in range(count)] for d in range(2, count, 2)]
    return [block] + [lax.ppermute(block, axis, shift) for shift in shifts]


def cell_rows(cells):
    first, second = cells[:, :, :HALF_LON], cells[:, :, HALF_LON:]
    rest = jnp.concatenate([first[:, :, HALF_MAIN:], second[:, :, HALF_MAIN:]], axis=2)
    main = jnp.concatenate([first[:, :, :HALF_MAIN], second[:, :, :HALF_MAIN]], axis=2)
    return jnp.concatenate([main, rest.reshape(J, 1, LAT_DEV * REST)], axis=1)


def shards(node_values, block_slot, cell_ref, cell_weight, target_spectrum, spec_weight):
    owners = lax.axis_size("band")
    band_index = lax.axis_index("band")
    samples, chans, nodes_local = node_values.shape
    lat_total = LAT_DEV * owners
    lat_weight = lat_weights(band_index * LAT_DEV, LAT_DEV, lat_total)
    table = jnp.asarray(dft_table())

    outgoing = pl.pallas_call(
        pack_kernel,
        out_shape=jax.ShapeDtypeStruct((owners, PAIR, NB), jnp.bfloat16),
        in_specs=[SMEM, VMEM],
        out_specs=VMEM,
        scratch_shapes=[pltpu.VMEM((owners, PAIR, NB), jnp.float32)],
        compiler_params=pltpu.CompilerParams(vmem_limit_bytes=60 * 1024 * 1024),
        name="pack",
    )(block_slot, node_values[0])
    outgoing, target_spectrum, cell_ref, cell_weight, spec_weight = lax.optimization_barrier(
        (outgoing, target_spectrum, cell_ref, cell_weight, spec_weight)
    )
    received = exchange(outgoing, "band")

    refs = cell_rows(cell_ref)
    weights = cell_rows(cell_weight)
    target = jnp.pad(
        jnp.transpose(target_spectrum[0].reshape(chans, LAT_DEV, 2 * K), (1, 0, 2)),
        ((0, 0), (0, CP - chans), (0, 0)),
    ).reshape(ROWS, 2 * K)

    true_part, energy_part = pl.pallas_call(
        true_kernel,
        out_shape=(
            jax.ShapeDtypeStruct((CP, K), jnp.float32),
            jax.ShapeDtypeStruct((8, 128), jnp.float32),
        ),
        in_specs=[SMEM, VMEM, VMEM],
        out_specs=(VMEM, VMEM),
        compiler_params=PARAMS,
        name="true_power",
    )(lat_weight, spec_weight[None, :], target)
    energies = everyone(energy_part, "chan")

    grid, energy = pl.pallas_call(
        functools.partial(gather_kernel, owners),
        out_shape=(
            jax.ShapeDtypeStruct((2 * ROWS, HALF_PAD), jnp.bfloat16),
            jax.ShapeDtypeStruct(energy_part.shape, jnp.float32),
        ),
        in_specs=[VMEM] * (3 + len(energies)),
        out_specs=(VMEM, VMEM),
        scratch_shapes=[
            pltpu.VMEM((owners * CHANS, LO), jnp.float32),
            pltpu.VMEM((owners * CHANS, LO), jnp.bfloat16),
            pltpu.VMEM((CELL_ROWS * CP, MAIN), jnp.bfloat16),
        ],
        compiler_params=PARAMS,
        name="gather",
    )(received, refs, weights, *energies)

    spectrum, sums = pl.pallas_call(
        spectrum_kernel,
        out_shape=(
            jax.ShapeDtypeStruct((ROWS, 2 * K), jnp.bfloat16),
            jax.ShapeDtypeStruct((CP, 1, 3 * K + NB), jnp.float32),
        ),
        in_specs=[SMEM] + [VMEM] * 5,
        out_specs=(VMEM, VMEM),
        compiler_params=PARAMS,
        name="spectrum",
    )(lat_weight, grid, table, target, true_part, energy)

    parts = exchange(sums, "band")
    factors = pl.pallas_call(
        functools.partial(middle_kernel, 1.0 / (C * K * lat_total)),
        out_shape=jax.ShapeDtypeStruct((owners, 1, 2 * K), jnp.float32),
        in_specs=[VMEM, VMEM],
        out_specs=VMEM,
        compiler_params=PARAMS,
        name="middle",
    )(parts, spec_weight[None, :])
    factors = exchange(factors, "band")

    slot_grad = pl.pallas_call(
        functools.partial(backward_kernel, owners),
        out_shape=jax.ShapeDtypeStruct((owners, PAIR, NB), jnp.bfloat16),
        in_specs=[SMEM] + [VMEM] * 6,
        out_specs=VMEM,
        scratch_shapes=[
            pltpu.VMEM((2 * ROWS, 2 * K), jnp.bfloat16),
            pltpu.VMEM((owners * CHANS, LO), jnp.float32),
            pltpu.VMEM((CELL_ROWS * CP, MAIN), jnp.float32),
        ],
        compiler_params=PARAMS,
        name="backward",
    )(lat_weight, refs, weights, table, target, spectrum, factors)

    returned = exchange(slot_grad, "band")
    node_grad = pl.pallas_call(
        unpack_kernel,
        out_shape=jax.ShapeDtypeStruct((chans, nodes_local), jnp.bfloat16),
        in_specs=[SMEM, VMEM],
        out_specs=VMEM,
        scratch_shapes=[pltpu.VMEM((owners, PAIR, NB), jnp.float32)],
        compiler_params=PARAMS,
        name="unpack",
    )(block_slot, returned)
    return node_grad[None]


def solution(mesh):
    in_specs = (
        P(None, "chan", "band"),
        P("band"),
        P(None, "band", None),
        P(None, "band", None),
        P(None, "chan", "band", None, None),
        P(),
    )
    out_specs = P(None, "chan", "band")
    return jax.shard_map(shards, mesh=mesh, in_specs=in_specs, out_specs=out_specs, check_vma=False)
```

```python
import functools
import math

import jax
import jax.numpy as jnp
import numpy as np
from jax import lax
from jax.experimental import pallas as pl
from jax.experimental.pallas import tpu as pltpu
from jax.sharding import PartitionSpec as P

C = 224
LON = 1440
K = 640
J = 3
NB = 128
LAT_DEV = 8
NBLK_DEV = 32
CAP = 2

HALF_LON = LON // 2
HALF_PAD = 768
TILE = 256
LO = CAP * NB
CP = 32
HALF_MAIN = 640
HALF_REST = HALF_LON - HALF_MAIN
MAIN = 2 * HALF_MAIN
REST = 2 * HALF_REST
CELL_ROWS = LAT_DEV + 1
CHANS = 28
HALF = 4
BODY = CHANS - HALF
PAIR = 2 * CHANS
ROWS = LAT_DEV * CP

epsilon = 1e-06


def dft_table():
    wavenumber = np.arange(K, dtype=np.int64)[:, None]
    column = np.arange(LON, dtype=np.int64)[None, :]
    phase_count = wavenumber * column % LON
    phase_angle = np.float32(2.0 * math.pi / LON) * phase_count.astype(np.float32)
    norm_factor = np.float32(1.0 / math.sqrt(LON))
    table = np.stack([np.cos(phase_angle) * norm_factor, -np.sin(phase_angle) * norm_factor])
    table = table.astype(jnp.bfloat16).reshape(2 * K, LON)[:, :HALF_LON]
    return np.pad(table, ((0, 0), (0, HALF_PAD - HALF_LON)))


def half_sign():
    wavenumber = lax.broadcasted_iota(jnp.int32, (1, 2 * K), 1)
    return jnp.where((wavenumber & 1) == 0, 1.0, -1.0)


def lat_weights(first_row, row_count, lat_total):
    row_index = first_row + jnp.arange(row_count, dtype=jnp.int32)
    latitude = (row_index.astype(jnp.float32) + 0.5) * (math.pi / lat_total) - 0.5 * math.pi
    return jnp.cos(latitude)


def first_rows(lanes):
    return lax.broadcasted_iota(jnp.int32, (2 * HALF, lanes), 0) < HALF


def pack_kernel(slot_ref, nodes_ref, out_ref, staged):
    staged[...] = jnp.zeros_like(staged)
    first = first_rows(NB)
    for i in range(NBLK_DEV):
        owner, slot = slot_ref[i] >> 1, slot_ref[i] & 1
        block = nodes_ref[:, i * NB : (i + 1) * NB].astype(jnp.float32)
        at = pl.multiple_of(slot * (BODY + 2 * HALF), 8)
        staged[owner, pl.ds(at, BODY), :] = block[:BODY]
        last = jnp.concatenate([block[BODY:], block[BODY:]], axis=0)
        shared = staged[owner, BODY : BODY + 2 * HALF, :]
        staged[owner, BODY : BODY + 2 * HALF, :] = jnp.where(first == (slot == 0), last, shared)
    out_ref[...] = staged[...].astype(jnp.bfloat16)


def unpack_kernel(slot_ref, blocks_ref, out_ref, staged):
    staged[...] = blocks_ref[...].astype(jnp.float32)
    for i in range(NBLK_DEV):
        owner, slot = slot_ref[i] >> 1, slot_ref[i] & 1
        at = pl.multiple_of(slot * (BODY + 2 * HALF), 8)
        body = staged[owner, pl.ds(at, BODY), :]
        shared = staged[owner, BODY : BODY + 2 * HALF, :]
        last = jnp.where(slot == 0, shared, pltpu.roll(shared, HALF, 0))[:HALF]
        block = jnp.concatenate([body, last], axis=0)
        out_ref[:, i * NB : (i + 1) * NB] = block.astype(jnp.bfloat16)


def true_kernel(lat_ref, spec_weight_ref, target_ref, true_ref, energy_ref):
    true = jnp.zeros((CP, 2 * K), jnp.float32)
    for a in range(LAT_DEV):
        g = target_ref[a * CP : (a + 1) * CP, :].astype(jnp.float32)
        true = true + lat_ref[a] * g * g
    true = true[:, :K] + true[:, K:]
    true_ref[...] = true
    energy = jnp.sum(true * spec_weight_ref[...], axis=(0, 1), keepdims=True)
    energy_ref[...] = jnp.broadcast_to(energy, energy_ref.shape)


def middle_kernel(scale, parts_ref, spec_weight_ref, out_ref):
    sums = jnp.sum(parts_ref[...], axis=0)
    pred_power, true_power, cross_sum = sums[:, :K], sums[:, K : 2 * K], sums[:, 2 * K : 3 * K]
    energy = sums[:, 3 * K : 3 * K + 1] * scale + epsilon
    loss_scale = spec_weight_ref[...] / energy
    amp_pred = jnp.sqrt(pred_power + epsilon)
    amp_true = jnp.sqrt(true_power + epsilon)
    d_pred = (
        loss_scale
        * (
            4.0 * amp_pred
            - 2.0 * amp_true
            - cross_sum * (1.0 / amp_true - amp_true / (amp_pred * amp_pred))
        )
        / (2.0 * amp_pred)
    )
    d_cross = -loss_scale * (amp_pred / amp_true + amp_true / amp_pred)
    both = jnp.concatenate([d_pred, d_cross], axis=1)
    out_ref[...] = jnp.broadcast_to(both[None], out_ref.shape)


def one_hot(ref_row):
    owner = ref_row >> 8
    place = ref_row & (LO - 1)
    rows = lax.broadcasted_iota(jnp.int32, (LO, ref_row.shape[1]), 0)
    return owner, (rows == place).astype(jnp.float32).astype(jnp.bfloat16)


def shared_owner(owner):
    first = lax.broadcasted_iota(jnp.int32, (2 * HALF, owner.shape[1]), 0) < HALF
    wanted = jnp.where(first, 0, 1)
    return jnp.where((owner & 1) == wanted, owner >> 1, -1)


def gather_kernel(owners, buf_ref, cell_ref, weight_ref, *refs):
    energy_refs = refs[:-5]
    grid_ref, energy_ref, staged, nodes, grid = refs[-5:]
    energy_ref[...] = sum((ref[...] for ref in energy_refs[1:]), energy_refs[0][...])
    first = first_rows(NB)
    for p in range(owners // 2):
        even = buf_ref[2 * p].astype(jnp.float32)
        odd = buf_ref[2 * p + 1].astype(jnp.float32)
        middle = slice(BODY, BODY + 2 * HALF)
        tail = slice(BODY + 2 * HALF, PAIR)
        at = p * PAIR
        staged[at : at + BODY, :NB], staged[at : at + BODY, NB:] = even[:BODY], even[tail]
        staged[at + BODY : at + BODY + 2 * HALF, :NB] = jnp.where(
            first, even[middle], pltpu.roll(odd[middle], HALF, 0)
        )
        staged[at + BODY : at + BODY + 2 * HALF, NB:] = jnp.where(
            first, pltpu.roll(even[middle], HALF, 0), odd[middle]
        )
        staged[at + BODY + 2 * HALF : at + PAIR, :NB] = odd[:BODY]
        staged[at + BODY + 2 * HALF : at + PAIR, NB:] = odd[tail]
    nodes[...] = staged[...].astype(jnp.bfloat16)

    def row(a, _):
        for t in range(MAIN // TILE):
            cols = slice(t * TILE, (t + 1) * TILE)
            total = jnp.zeros((CP, TILE), jnp.float32)
            for m in range(J):
                owner, hot = one_hot(cell_ref[m, pl.ds(a, 1), cols])
                shared = shared_owner(owner)
                picked = jnp.dot(nodes[...], hot, preferred_element_type=jnp.float32)
                body = jnp.zeros((BODY, TILE), jnp.float32)
                half = jnp.zeros((2 * HALF, TILE), jnp.float32)
                for p in range(owners // 2):
                    block = picked[p * PAIR : (p + 1) * PAIR]
                    body = jnp.where(owner == 2 * p, block[:BODY], body)
                    half = jnp.where(shared == p, block[BODY : BODY + 2 * HALF], half)
                    body = jnp.where(owner == 2 * p + 1, block[BODY + 2 * HALF :], body)
                value = jnp.concatenate([body, half + pltpu.roll(half, HALF, 0)], axis=0)
                total = total + weight_ref[m, pl.ds(a, 1), cols] * value
            grid[pl.ds(pl.multiple_of(a * CP, CP), CP), cols] = total.astype(jnp.bfloat16)
        return 0

    lax.fori_loop(0, CELL_ROWS, row, 0, unroll=3)
    rest = grid[ROWS : ROWS + CP, :].astype(jnp.float32)
    zeros = jnp.zeros((CP, HALF_PAD - HALF_LON), jnp.float32)
    for a in range(LAT_DEV):
        for h in range(2):
            at = a * REST + h * HALF_REST
            piece = jnp.concatenate([rest[:, at : at + HALF_REST], zeros], axis=1)
            rows = slice(h * ROWS + a * CP, h * ROWS + (a + 1) * CP)
            grid_ref[rows, HALF_MAIN:] = piece.astype(jnp.bfloat16)
    for h in range(2):
        columns = slice(h * HALF_MAIN, (h + 1) * HALF_MAIN)
        grid_ref[h * ROWS : (h + 1) * ROWS, :HALF_MAIN] = grid[:ROWS, columns]


def spectrum_kernel(lat_ref, grid_ref, table_ref, target_ref, true_ref, energy_ref, spec_ref,
                    sums_ref):
    halves = lax.dot_general(
        grid_ref[...], table_ref[...], (((1,), (1,)), ((), ())),
        preferred_element_type=jnp.float32,
    )
    spectrum = halves[:ROWS] + half_sign() * halves[ROWS:]
    spec_ref[...] = spectrum.astype(jnp.bfloat16)
    pred = jnp.zeros((CP, 2 * K), jnp.float32)
    cross = jnp.zeros((CP, 2 * K), jnp.float32)
    for a in range(LAT_DEV):
        s = spec_ref[a * CP : (a + 1) * CP, :].astype(jnp.float32)
        g = target_ref[a * CP : (a + 1) * CP, :].astype(jnp.float32)
        ws = lat_ref[a] * s
        pred = pred + ws * s
        cross = cross + ws * g
    sums_ref[:, 0, :K] = pred[:, :K] + pred[:, K:]
    sums_ref[:, 0, K : 2 * K] = true_ref[...]
    sums_ref[:, 0, 2 * K : 3 * K] = cross[:, :K] + cross[:, K:]
    sums_ref[:, 0, 3 * K :] = jnp.broadcast_to(energy_ref[0:1, :], (CP, NB))


def backward_kernel(owners, lat_ref, cell_ref, weight_ref, table_ref, target_ref, spec_ref,
                    factor_ref, out_ref, grads, total, gated):
    d_pred, d_cross = factor_ref[:, 0, :K], factor_ref[:, 0, K:]
    sign = half_sign()[:, :K]
    for a in range(LAT_DEV):
        rows = slice(a * CP, (a + 1) * CP)
        for r in range(2):
            cols = slice(r * K, (r + 1) * K)
            s = spec_ref[rows, cols].astype(jnp.float32)
            g = target_ref[rows, cols].astype(jnp.float32)
            grad = lat_ref[a] * (2.0 * s * d_pred + g * d_cross)
            grads[rows, cols] = grad.astype(jnp.bfloat16)
            flipped = slice(ROWS + a * CP, ROWS + (a + 1) * CP)
            grads[flipped, cols] = (grad * sign).astype(jnp.bfloat16)
    grid_grad = jnp.dot(grads[...], table_ref[...], preferred_element_type=jnp.float32)
    rest = []
    for h in range(2):
        columns = slice(h * HALF_MAIN, (h + 1) * HALF_MAIN)
        gated[:ROWS, columns] = grid_grad[h * ROWS : (h + 1) * ROWS, :HALF_MAIN]
    for a in range(LAT_DEV):
        for h in range(2):
            rows = slice(h * ROWS + a * CP, h * ROWS + (a + 1) * CP)
            rest.append(grid_grad[rows, HALF_MAIN:HALF_LON])
    gated[ROWS:, :] = jnp.concatenate(rest, axis=1)
    total[...] = jnp.zeros_like(total)

    def row(a, _):
        for t in range(MAIN // TILE):
            cols = slice(t * TILE, (t + 1) * TILE)
            value = gated[pl.ds(pl.multiple_of(a * CP, CP), CP), cols]
            for m in range(J):
                owner, hot = one_hot(cell_ref[m, pl.ds(a, 1), cols])
                shared = shared_owner(owner)
                part = weight_ref[m, pl.ds(a, 1), cols] * value
                body, last = part[:BODY], part[BODY:]
                first = lax.broadcasted_iota(jnp.int32, last.shape, 0) < HALF
                half = jnp.where(first, last, pltpu.roll(last, HALF, 0))
                pieces = []
                for p in range(owners // 2):
                    pieces.append(jnp.where(owner == 2 * p, body, 0.0))
                    pieces.append(jnp.where(shared == p, half, 0.0))
                    pieces.append(jnp.where(owner == 2 * p + 1, body, 0.0))
                spread = jnp.concatenate(pieces, axis=0).astype(jnp.bfloat16)
                total[...] += lax.dot_general(
                    spread, hot, (((1,), (1,)), ((), ())), preferred_element_type=jnp.float32
                )
        return 0

    lax.fori_loop(0, CELL_ROWS, row, 0, unroll=3)
    first = first_rows(NB)
    for p in range(owners // 2):
        block = total[p * PAIR : (p + 1) * PAIR, :]
        left, right = block[BODY : BODY + 2 * HALF, :NB], block[BODY : BODY + 2 * HALF, NB:]
        even = jnp.where(first, left, pltpu.roll(right, HALF, 0))
        odd = jnp.where(first, pltpu.roll(left, HALF, 0), right)
        body = block[:BODY]
        out_ref[2 * p] = jnp.concatenate([body[:, :NB], even, body[:, NB:]], axis=0).astype(
            jnp.bfloat16
        )
        body = block[BODY + 2 * HALF :]
        out_ref[2 * p + 1] = jnp.concatenate([body[:, :NB], odd, body[:, NB:]], axis=0).astype(
            jnp.bfloat16
        )


SMEM = pl.BlockSpec(memory_space=pltpu.SMEM)
VMEM = pl.BlockSpec(memory_space=pltpu.VMEM)
PARAMS = pltpu.CompilerParams(vmem_limit_bytes=24 * 1024 * 1024)


def exchange(blocks, axis):
    return lax.all_to_all(blocks, axis, split_axis=0, concat_axis=0, tiled=True)


def everyone(block, axis):
    count = lax.axis_size(axis)
    block = block + lax.ppermute(block, axis, [(i, i ^ 1) for i in range(count)])
    shifts = [[(i, (i + d) % count) for i in range(count)] for d in range(2, count, 2)]
    return [block] + [lax.ppermute(block, axis, shift) for shift in shifts]


def cell_rows(cells):
    first, second = cells[:, :, :HALF_LON], cells[:, :, HALF_LON:]
    rest = jnp.concatenate([first[:, :, HALF_MAIN:], second[:, :, HALF_MAIN:]], axis=2)
    main = jnp.concatenate([first[:, :, :HALF_MAIN], second[:, :, :HALF_MAIN]], axis=2)
    return jnp.concatenate([main, rest.reshape(J, 1, LAT_DEV * REST)], axis=1)


def shards(node_values, block_slot, cell_ref, cell_weight, target_spectrum, spec_weight):
    owners = lax.axis_size("band")
    band_index = lax.axis_index("band")
    samples, chans, nodes_local = node_values.shape
    lat_total = LAT_DEV * owners
    lat_weight = lat_weights(band_index * LAT_DEV, LAT_DEV, lat_total)
    table = jnp.asarray(dft_table())

    outgoing = pl.pallas_call(
        pack_kernel,
        out_shape=jax.ShapeDtypeStruct((owners, PAIR, NB), jnp.bfloat16),
        in_specs=[SMEM, VMEM],
        out_specs=VMEM,
        scratch_shapes=[pltpu.VMEM((owners, PAIR, NB), jnp.float32)],
        compiler_params=pltpu.CompilerParams(vmem_limit_bytes=60 * 1024 * 1024),
        name="pack",
    )(block_slot, node_values[0])
    outgoing, target_spectrum, cell_ref, cell_weight, spec_weight = lax.optimization_barrier(
        (outgoing, target_spectrum, cell_ref, cell_weight, spec_weight)
    )
    received = exchange(outgoing, "band")

    refs = cell_rows(cell_ref)
    weights = cell_rows(cell_weight)
    target = jnp.pad(
        jnp.transpose(target_spectrum[0].reshape(chans, LAT_DEV, 2 * K), (1, 0, 2)),
        ((0, 0), (0, CP - chans), (0, 0)),
    ).reshape(ROWS, 2 * K)

    true_part, energy_part = pl.pallas_call(
        true_kernel,
        out_shape=(
            jax.ShapeDtypeStruct((CP, K), jnp.float32),
            jax.ShapeDtypeStruct((8, 128), jnp.float32),
        ),
        in_specs=[SMEM, VMEM, VMEM],
        out_specs=(VMEM, VMEM),
        compiler_params=PARAMS,
        name="true_power",
    )(lat_weight, spec_weight[None, :], target)
    energies = everyone(energy_part, "chan")

    grid, energy = pl.pallas_call(
        functools.partial(gather_kernel, owners),
        out_shape=(
            jax.ShapeDtypeStruct((2 * ROWS, HALF_PAD), jnp.bfloat16),
            jax.ShapeDtypeStruct(energy_part.shape, jnp.float32),
        ),
        in_specs=[VMEM] * (3 + len(energies)),
        out_specs=(VMEM, VMEM),
        scratch_shapes=[
            pltpu.VMEM((owners * CHANS, LO), jnp.float32),
            pltpu.VMEM((owners * CHANS, LO), jnp.bfloat16),
            pltpu.VMEM((CELL_ROWS * CP, MAIN), jnp.bfloat16),
        ],
        compiler_params=PARAMS,
        name="gather",
    )(received, refs, weights, *energies)

    spectrum, sums = pl.pallas_call(
        spectrum_kernel,
        out_shape=(
            jax.ShapeDtypeStruct((ROWS, 2 * K), jnp.bfloat16),
            jax.ShapeDtypeStruct((CP, 1, 3 * K + NB), jnp.float32),
        ),
        in_specs=[SMEM] + [VMEM] * 5,
        out_specs=(VMEM, VMEM),
        compiler_params=PARAMS,
        name="spectrum",
    )(lat_weight, grid, table, target, true_part, energy)

    parts = exchange(sums, "band")
    factors = pl.pallas_call(
        functools.partial(middle_kernel, 1.0 / (C * K * lat_total)),
        out_shape=jax.ShapeDtypeStruct((owners, 1, 2 * K), jnp.float32),
        in_specs=[VMEM, VMEM],
        out_specs=VMEM,
        compiler_params=PARAMS,
        name="middle",
    )(parts, spec_weight[None, :])
    factors = exchange(factors, "band")

    slot_grad = pl.pallas_call(
        functools.partial(backward_kernel, owners),
        out_shape=jax.ShapeDtypeStruct((owners, PAIR, NB), jnp.bfloat16),
        in_specs=[SMEM] + [VMEM] * 6,
        out_specs=VMEM,
        scratch_shapes=[
            pltpu.VMEM((2 * ROWS, 2 * K), jnp.bfloat16),
            pltpu.VMEM((owners * CHANS, LO), jnp.float32),
            pltpu.VMEM((CELL_ROWS * CP, MAIN), jnp.float32),
        ],
        compiler_params=PARAMS,
        name="backward",
    )(lat_weight, refs, weights, table, target, spectrum, factors)

    returned = exchange(slot_grad, "band")
    node_grad = pl.pallas_call(
        unpack_kernel,
        out_shape=jax.ShapeDtypeStruct((chans, nodes_local), jnp.bfloat16),
        in_specs=[SMEM, VMEM],
        out_specs=VMEM,
        scratch_shapes=[pltpu.VMEM((owners, PAIR, NB), jnp.float32)],
        compiler_params=PARAMS,
        name="unpack",
    )(block_slot, returned)
    return node_grad[None]


def solution(mesh):
    in_specs = (
        P(None, "chan", "band"),
        P("band"),
        P(None, "band", None),
        P(None, "band", None),
        P(None, "chan", "band", None, None),
        P(),
    )
    out_specs = P(None, "chan", "band")
    return jax.shard_map(shards, mesh=mesh, in_specs=in_specs, out_specs=out_specs, check_vma=False)
```

```python
import functools
import math

import jax
import jax.numpy as jnp
import numpy as np
from jax import lax
from jax.experimental import pallas as pl
from jax.experimental.pallas import tpu as pltpu
from jax.sharding import PartitionSpec as P

C = 224
LON = 1440
K = 640
J = 3
NB = 128
LAT_DEV = 8
NBLK_DEV = 32
CAP = 2

HALF_LON = LON // 2
HALF_PAD = 768
TILE = 256
LO = CAP * NB
CP = 32
HALF_MAIN = 640
HALF_REST = HALF_LON - HALF_MAIN
MAIN = 2 * HALF_MAIN
REST = 2 * HALF_REST
CELL_ROWS = LAT_DEV + 1
CHANS = 28
HALF = 4
BODY = CHANS - HALF
PAIR = 2 * CHANS
ROWS = LAT_DEV * CP

epsilon = 1e-06


def dft_table():
    wavenumber = np.arange(K, dtype=np.int64)[:, None]
    column = np.arange(LON, dtype=np.int64)[None, :]
    phase_count = wavenumber * column % LON
    phase_angle = np.float32(2.0 * math.pi / LON) * phase_count.astype(np.float32)
    norm_factor = np.float32(1.0 / math.sqrt(LON))
    table = np.stack([np.cos(phase_angle) * norm_factor, -np.sin(phase_angle) * norm_factor])
    table = table.astype(jnp.bfloat16).reshape(2 * K, LON)[:, :HALF_LON]
    return np.pad(table, ((0, 0), (0, HALF_PAD - HALF_LON)))


def half_sign():
    wavenumber = lax.broadcasted_iota(jnp.int32, (1, 2 * K), 1)
    return jnp.where((wavenumber & 1) == 0, 1.0, -1.0)


def lat_weights(first_row, row_count, lat_total):
    row_index = first_row + jnp.arange(row_count, dtype=jnp.int32)
    latitude = (row_index.astype(jnp.float32) + 0.5) * (math.pi / lat_total) - 0.5 * math.pi
    return jnp.cos(latitude)


def first_rows(lanes):
    return lax.broadcasted_iota(jnp.int32, (2 * HALF, lanes), 0) < HALF


def pack_kernel(slot_ref, nodes_ref, out_ref, staged):
    staged[...] = jnp.zeros_like(staged)
    first = first_rows(NB)
    for i in range(NBLK_DEV):
        owner, slot = slot_ref[i] >> 1, slot_ref[i] & 1
        block = nodes_ref[:, i * NB : (i + 1) * NB].astype(jnp.float32)
        at = pl.multiple_of(slot * (BODY + 2 * HALF), 8)
        staged[owner, pl.ds(at, BODY), :] = block[:BODY]
        last = jnp.concatenate([block[BODY:], block[BODY:]], axis=0)
        shared = staged[owner, BODY : BODY + 2 * HALF, :]
        staged[owner, BODY : BODY + 2 * HALF, :] = jnp.where(first == (slot == 0), last, shared)
    out_ref[...] = staged[...].astype(jnp.bfloat16)


def unpack_kernel(slot_ref, blocks_ref, out_ref, staged):
    staged[...] = blocks_ref[...].astype(jnp.float32)
    for i in range(NBLK_DEV):
        owner, slot = slot_ref[i] >> 1, slot_ref[i] & 1
        at = pl.multiple_of(slot * (BODY + 2 * HALF), 8)
        body = staged[owner, pl.ds(at, BODY), :]
        shared = staged[owner, BODY : BODY + 2 * HALF, :]
        last = jnp.where(slot == 0, shared, pltpu.roll(shared, HALF, 0))[:HALF]
        block = jnp.concatenate([body, last], axis=0)
        out_ref[:, i * NB : (i + 1) * NB] = block.astype(jnp.bfloat16)


def true_kernel(lat_ref, spec_weight_ref, target_ref, true_ref, energy_ref):
    true = jnp.zeros((CP, 2 * K), jnp.float32)
    for a in range(LAT_DEV):
        g = target_ref[a * CP : (a + 1) * CP, :].astype(jnp.float32)
        true = true + lat_ref[a] * g * g
    true = true[:, :K] + true[:, K:]
    true_ref[...] = true
    energy = jnp.sum(true * spec_weight_ref[...], axis=(0, 1), keepdims=True)
    energy_ref[...] = jnp.broadcast_to(energy, energy_ref.shape)


def middle_kernel(scale, parts_ref, spec_weight_ref, out_ref):
    sums = jnp.sum(parts_ref[...], axis=0)
    pred_power, true_power, cross_sum = sums[:, :K], sums[:, K : 2 * K], sums[:, 2 * K : 3 * K]
    energy = sums[:, 3 * K : 3 * K + 1] * scale + epsilon
    loss_scale = spec_weight_ref[...] / energy
    amp_pred = jnp.sqrt(pred_power + epsilon)
    amp_true = jnp.sqrt(true_power + epsilon)
    d_pred = (
        loss_scale
        * (
            4.0 * amp_pred
            - 2.0 * amp_true
            - cross_sum * (1.0 / amp_true - amp_true / (amp_pred * amp_pred))
        )
        / (2.0 * amp_pred)
    )
    d_cross = -loss_scale * (amp_pred / amp_true + amp_true / amp_pred)
    both = jnp.concatenate([d_pred, d_cross], axis=1)
    out_ref[...] = jnp.broadcast_to(both[None], out_ref.shape)


def one_hot(ref_row):
    owner = ref_row >> 8
    place = ref_row & (LO - 1)
    rows = lax.broadcasted_iota(jnp.int32, (LO, ref_row.shape[1]), 0)
    return owner, (rows == place).astype(jnp.float32).astype(jnp.bfloat16)


def shared_owner(owner):
    first = lax.broadcasted_iota(jnp.int32, (2 * HALF, owner.shape[1]), 0) < HALF
    wanted = jnp.where(first, 0, 1)
    return jnp.where((owner & 1) == wanted, owner >> 1, -1)


def forward_kernel(owners, lat_ref, buf_ref, cell_ref, weight_ref, table_ref, target_ref,
                   true_ref, *refs):
    energy_refs = refs[:-6]
    spec_ref, sums_ref, staged, nodes, grid, half_rows = refs[-6:]
    first = first_rows(NB)
    for p in range(owners // 2):
        even = buf_ref[2 * p].astype(jnp.float32)
        odd = buf_ref[2 * p + 1].astype(jnp.float32)
        middle = slice(BODY, BODY + 2 * HALF)
        tail = slice(BODY + 2 * HALF, PAIR)
        at = p * PAIR
        staged[at : at + BODY, :NB], staged[at : at + BODY, NB:] = even[:BODY], even[tail]
        staged[at + BODY : at + BODY + 2 * HALF, :NB] = jnp.where(
            first, even[middle], pltpu.roll(odd[middle], HALF, 0)
        )
        staged[at + BODY : at + BODY + 2 * HALF, NB:] = jnp.where(
            first, pltpu.roll(even[middle], HALF, 0), odd[middle]
        )
        staged[at + BODY + 2 * HALF : at + PAIR, :NB] = odd[:BODY]
        staged[at + BODY + 2 * HALF : at + PAIR, NB:] = odd[tail]
    nodes[...] = staged[...].astype(jnp.bfloat16)

    def row(a, _):
        for t in range(MAIN // TILE):
            cols = slice(t * TILE, (t + 1) * TILE)
            total = jnp.zeros((CP, TILE), jnp.float32)
            for m in range(J):
                owner, hot = one_hot(cell_ref[m, pl.ds(a, 1), cols])
                shared = shared_owner(owner)
                picked = jnp.dot(nodes[...], hot, preferred_element_type=jnp.float32)
                body = jnp.zeros((BODY, TILE), jnp.float32)
                half = jnp.zeros((2 * HALF, TILE), jnp.float32)
                for p in range(owners // 2):
                    block = picked[p * PAIR : (p + 1) * PAIR]
                    body = jnp.where(owner == 2 * p, block[:BODY], body)
                    half = jnp.where(shared == p, block[BODY : BODY + 2 * HALF], half)
                    body = jnp.where(owner == 2 * p + 1, block[BODY + 2 * HALF :], body)
                value = jnp.concatenate([body, half + pltpu.roll(half, HALF, 0)], axis=0)
                total = total + weight_ref[m, pl.ds(a, 1), cols] * value
            grid[pl.ds(pl.multiple_of(a * CP, CP), CP), cols] = total.astype(jnp.bfloat16)
        return 0

    lax.fori_loop(0, CELL_ROWS, row, 0, unroll=3)
    rest = grid[ROWS : ROWS + CP, :].astype(jnp.float32)
    zeros = jnp.zeros((CP, HALF_PAD - HALF_LON), jnp.float32)
    for a in range(LAT_DEV):
        for h in range(2):
            at = a * REST + h * HALF_REST
            piece = jnp.concatenate([rest[:, at : at + HALF_REST], zeros], axis=1)
            rows = slice(h * ROWS + a * CP, h * ROWS + (a + 1) * CP)
            half_rows[rows, HALF_MAIN:] = piece.astype(jnp.bfloat16)
    for h in range(2):
        columns = slice(h * HALF_MAIN, (h + 1) * HALF_MAIN)
        half_rows[h * ROWS : (h + 1) * ROWS, :HALF_MAIN] = grid[:ROWS, columns]
    halves = lax.dot_general(
        half_rows[...], table_ref[...], (((1,), (1,)), ((), ())),
        preferred_element_type=jnp.float32,
    )
    spectrum = halves[:ROWS] + half_sign() * halves[ROWS:]
    spec_ref[...] = spectrum.astype(jnp.bfloat16)
    pred = jnp.zeros((CP, 2 * K), jnp.float32)
    cross = jnp.zeros((CP, 2 * K), jnp.float32)
    for a in range(LAT_DEV):
        s = spec_ref[a * CP : (a + 1) * CP, :].astype(jnp.float32)
        g = target_ref[a * CP : (a + 1) * CP, :].astype(jnp.float32)
        ws = lat_ref[a] * s
        pred = pred + ws * s
        cross = cross + ws * g
    sums_ref[:, 0, :K] = pred[:, :K] + pred[:, K:]
    sums_ref[:, 0, K : 2 * K] = true_ref[...]
    sums_ref[:, 0, 2 * K : 3 * K] = cross[:, :K] + cross[:, K:]
    energy = sum((ref[0:1, :] for ref in energy_refs[1:]), energy_refs[0][0:1, :])
    sums_ref[:, 0, 3 * K :] = jnp.broadcast_to(energy, (CP, NB))


def backward_kernel(owners, lat_ref, cell_ref, weight_ref, table_ref, target_ref, spec_ref,
                    factor_ref, out_ref, grads, total, gated):
    d_pred, d_cross = factor_ref[:, 0, :K], factor_ref[:, 0, K:]
    sign = half_sign()[:, :K]
    for a in range(LAT_DEV):
        rows = slice(a * CP, (a + 1) * CP)
        for r in range(2):
            cols = slice(r * K, (r + 1) * K)
            s = spec_ref[rows, cols].astype(jnp.float32)
            g = target_ref[rows, cols].astype(jnp.float32)
            grad = lat_ref[a] * (2.0 * s * d_pred + g * d_cross)
            grads[rows, cols] = grad.astype(jnp.bfloat16)
            flipped = slice(ROWS + a * CP, ROWS + (a + 1) * CP)
            grads[flipped, cols] = (grad * sign).astype(jnp.bfloat16)
    grid_grad = jnp.dot(grads[...], table_ref[...], preferred_element_type=jnp.float32)
    rest = []
    for h in range(2):
        columns = slice(h * HALF_MAIN, (h + 1) * HALF_MAIN)
        gated[:ROWS, columns] = grid_grad[h * ROWS : (h + 1) * ROWS, :HALF_MAIN]
    for a in range(LAT_DEV):
        for h in range(2):
            rows = slice(h * ROWS + a * CP, h * ROWS + (a + 1) * CP)
            rest.append(grid_grad[rows, HALF_MAIN:HALF_LON])
    gated[ROWS:, :] = jnp.concatenate(rest, axis=1)
    total[...] = jnp.zeros_like(total)

    def row(a, _):
        for t in range(MAIN // TILE):
            cols = slice(t * TILE, (t + 1) * TILE)
            value = gated[pl.ds(pl.multiple_of(a * CP, CP), CP), cols]
            for m in range(J):
                owner, hot = one_hot(cell_ref[m, pl.ds(a, 1), cols])
                shared = shared_owner(owner)
                part = weight_ref[m, pl.ds(a, 1), cols] * value
                body, last = part[:BODY], part[BODY:]
                first = lax.broadcasted_iota(jnp.int32, last.shape, 0) < HALF
                half = jnp.where(first, last, pltpu.roll(last, HALF, 0))
                pieces = []
                for p in range(owners // 2):
                    pieces.append(jnp.where(owner == 2 * p, body, 0.0))
                    pieces.append(jnp.where(shared == p, half, 0.0))
                    pieces.append(jnp.where(owner == 2 * p + 1, body, 0.0))
                spread = jnp.concatenate(pieces, axis=0).astype(jnp.bfloat16)
                total[...] += lax.dot_general(
                    spread, hot, (((1,), (1,)), ((), ())), preferred_element_type=jnp.float32
                )
        return 0

    lax.fori_loop(0, CELL_ROWS, row, 0, unroll=3)
    first = first_rows(NB)
    for p in range(owners // 2):
        block = total[p * PAIR : (p + 1) * PAIR, :]
        left, right = block[BODY : BODY + 2 * HALF, :NB], block[BODY : BODY + 2 * HALF, NB:]
        even = jnp.where(first, left, pltpu.roll(right, HALF, 0))
        odd = jnp.where(first, pltpu.roll(left, HALF, 0), right)
        body = block[:BODY]
        out_ref[2 * p] = jnp.concatenate([body[:, :NB], even, body[:, NB:]], axis=0).astype(
            jnp.bfloat16
        )
        body = block[BODY + 2 * HALF :]
        out_ref[2 * p + 1] = jnp.concatenate([body[:, :NB], odd, body[:, NB:]], axis=0).astype(
            jnp.bfloat16
        )


SMEM = pl.BlockSpec(memory_space=pltpu.SMEM)
VMEM = pl.BlockSpec(memory_space=pltpu.VMEM)
PARAMS = pltpu.CompilerParams(vmem_limit_bytes=24 * 1024 * 1024)


def exchange(blocks, axis):
    return lax.all_to_all(blocks, axis, split_axis=0, concat_axis=0, tiled=True)


def everyone(block, axis):
    count = lax.axis_size(axis)
    block = block + lax.ppermute(block, axis, [(i, i ^ 1) for i in range(count)])
    shifts = [[(i, (i + d) % count) for i in range(count)] for d in range(2, count, 2)]
    return [block] + [lax.ppermute(block, axis, shift) for shift in shifts]


def cell_rows(cells):
    first, second = cells[:, :, :HALF_LON], cells[:, :, HALF_LON:]
    rest = jnp.concatenate([first[:, :, HALF_MAIN:], second[:, :, HALF_MAIN:]], axis=2)
    main = jnp.concatenate([first[:, :, :HALF_MAIN], second[:, :, :HALF_MAIN]], axis=2)
    return jnp.concatenate([main, rest.reshape(J, 1, LAT_DEV * REST)], axis=1)


def shards(node_values, block_slot, cell_ref, cell_weight, target_spectrum, spec_weight):
    owners = lax.axis_size("band")
    band_index = lax.axis_index("band")
    samples, chans, nodes_local = node_values.shape
    lat_total = LAT_DEV * owners
    lat_weight = lat_weights(band_index * LAT_DEV, LAT_DEV, lat_total)
    table = jnp.asarray(dft_table())

    outgoing = pl.pallas_call(
        pack_kernel,
        out_shape=jax.ShapeDtypeStruct((owners, PAIR, NB), jnp.bfloat16),
        in_specs=[SMEM, VMEM],
        out_specs=VMEM,
        scratch_shapes=[pltpu.VMEM((owners, PAIR, NB), jnp.float32)],
        compiler_params=pltpu.CompilerParams(vmem_limit_bytes=60 * 1024 * 1024),
        name="pack",
    )(block_slot, node_values[0])
    outgoing, target_spectrum, cell_ref, cell_weight, spec_weight = lax.optimization_barrier(
        (outgoing, target_spectrum, cell_ref, cell_weight, spec_weight)
    )
    received = exchange(outgoing, "band")

    refs = cell_rows(cell_ref)
    weights = cell_rows(cell_weight)
    target = jnp.pad(
        jnp.transpose(target_spectrum[0].reshape(chans, LAT_DEV, 2 * K), (1, 0, 2)),
        ((0, 0), (0, CP - chans), (0, 0)),
    ).reshape(ROWS, 2 * K)

    true_part, energy_part = pl.pallas_call(
        true_kernel,
        out_shape=(
            jax.ShapeDtypeStruct((CP, K), jnp.float32),
            jax.ShapeDtypeStruct((8, 128), jnp.float32),
        ),
        in_specs=[SMEM, VMEM, VMEM],
        out_specs=(VMEM, VMEM),
        compiler_params=PARAMS,
        name="true_power",
    )(lat_weight, spec_weight[None, :], target)
    energies = everyone(energy_part, "chan")

    spectrum, sums = pl.pallas_call(
        functools.partial(forward_kernel, owners),
        out_shape=(
            jax.ShapeDtypeStruct((ROWS, 2 * K), jnp.bfloat16),
            jax.ShapeDtypeStruct((CP, 1, 3 * K + NB), jnp.float32),
        ),
        in_specs=[SMEM] + [VMEM] * (6 + len(energies)),
        out_specs=(VMEM, VMEM),
        scratch_shapes=[
            pltpu.VMEM((owners * CHANS, LO), jnp.float32),
            pltpu.VMEM((owners * CHANS, LO), jnp.bfloat16),
            pltpu.VMEM((CELL_ROWS * CP, MAIN), jnp.bfloat16),
            pltpu.VMEM((2 * ROWS, HALF_PAD), jnp.bfloat16),
        ],
        compiler_params=PARAMS,
        name="forward",
    )(lat_weight, received, refs, weights, table, target, true_part, *energies)

    parts = exchange(sums, "band")
    factors = pl.pallas_call(
        functools.partial(middle_kernel, 1.0 / (C * K * lat_total)),
        out_shape=jax.ShapeDtypeStruct((owners, 1, 2 * K), jnp.float32),
        in_specs=[VMEM, VMEM],
        out_specs=VMEM,
        compiler_params=PARAMS,
        name="middle",
    )(parts, spec_weight[None, :])
    factors = exchange(factors, "band")

    slot_grad = pl.pallas_call(
        functools.partial(backward_kernel, owners),
        out_shape=jax.ShapeDtypeStruct((owners, PAIR, NB), jnp.bfloat16),
        in_specs=[SMEM] + [VMEM] * 6,
        out_specs=VMEM,
        scratch_shapes=[
            pltpu.VMEM((2 * ROWS, 2 * K), jnp.bfloat16),
            pltpu.VMEM((owners * CHANS, LO), jnp.float32),
            pltpu.VMEM((CELL_ROWS * CP, MAIN), jnp.float32),
        ],
        compiler_params=PARAMS,
        name="backward",
    )(lat_weight, refs, weights, table, target, spectrum, factors)

    returned = exchange(slot_grad, "band")
    node_grad = pl.pallas_call(
        unpack_kernel,
        out_shape=jax.ShapeDtypeStruct((chans, nodes_local), jnp.bfloat16),
        in_specs=[SMEM, VMEM],
        out_specs=VMEM,
        scratch_shapes=[pltpu.VMEM((owners, PAIR, NB), jnp.float32)],
        compiler_params=PARAMS,
        name="unpack",
    )(block_slot, returned)
    return node_grad[None]


def solution(mesh):
    in_specs = (
        P(None, "chan", "band"),
        P("band"),
        P(None, "band", None),
        P(None, "band", None),
        P(None, "chan", "band", None, None),
        P(),
    )
    out_specs = P(None, "chan", "band")
    return jax.shard_map(shards, mesh=mesh, in_specs=in_specs, out_specs=out_specs, check_vma=False)
```

```python
import functools
import math

import jax
import jax.numpy as jnp
import numpy as np
from jax import lax
from jax.experimental import pallas as pl
from jax.experimental.pallas import tpu as pltpu
from jax.sharding import PartitionSpec as P

C = 224
LON = 1440
K = 640
J = 3
NB = 128
LAT_DEV = 8
NBLK_DEV = 32
CAP = 2

HALF_LON = LON // 2
HALF_PAD = 768
TILE = 256
LO = CAP * NB
CP = 32
HALF_MAIN = 640
HALF_REST = HALF_LON - HALF_MAIN
MAIN = 2 * HALF_MAIN
REST = 2 * HALF_REST
CELL_ROWS = LAT_DEV + 1
CHANS = 28
HALF = 4
BODY = CHANS - HALF
PAIR = 2 * CHANS
ROWS = LAT_DEV * CP

epsilon = 1e-06


def dft_table():
    wavenumber = np.arange(K, dtype=np.int64)[:, None]
    column = np.arange(LON, dtype=np.int64)[None, :]
    phase_count = wavenumber * column % LON
    phase_angle = np.float32(2.0 * math.pi / LON) * phase_count.astype(np.float32)
    norm_factor = np.float32(1.0 / math.sqrt(LON))
    table = np.stack([np.cos(phase_angle) * norm_factor, -np.sin(phase_angle) * norm_factor])
    table = table.astype(jnp.bfloat16).reshape(2 * K, LON)[:, :HALF_LON]
    return np.pad(table, ((0, 0), (0, HALF_PAD - HALF_LON)))


def half_sign():
    wavenumber = lax.broadcasted_iota(jnp.int32, (1, 2 * K), 1)
    return jnp.where((wavenumber & 1) == 0, 1.0, -1.0)


def lat_weights(first_row, row_count, lat_total):
    row_index = first_row + jnp.arange(row_count, dtype=jnp.int32)
    latitude = (row_index.astype(jnp.float32) + 0.5) * (math.pi / lat_total) - 0.5 * math.pi
    return jnp.cos(latitude)


def first_rows(lanes):
    return lax.broadcasted_iota(jnp.int32, (2 * HALF, lanes), 0) < HALF


def pack_kernel(slot_ref, nodes_ref, out_ref, staged):
    staged[...] = jnp.zeros_like(staged)
    first = first_rows(NB)
    for i in range(NBLK_DEV):
        owner, slot = slot_ref[i] >> 1, slot_ref[i] & 1
        block = nodes_ref[:, i * NB : (i + 1) * NB].astype(jnp.float32)
        at = pl.multiple_of(slot * (BODY + 2 * HALF), 8)
        staged[owner, pl.ds(at, BODY), :] = block[:BODY]
        last = jnp.concatenate([block[BODY:], block[BODY:]], axis=0)
        shared = staged[owner, BODY : BODY + 2 * HALF, :]
        staged[owner, BODY : BODY + 2 * HALF, :] = jnp.where(first == (slot == 0), last, shared)
    out_ref[...] = staged[...].astype(jnp.bfloat16)


def unpack_kernel(slot_ref, blocks_ref, out_ref):
    for i in range(NBLK_DEV):
        owner, slot = slot_ref[i] >> 1, slot_ref[i] & 1
        rows = blocks_ref[owner].astype(jnp.float32)
        shared = rows[BODY : BODY + 2 * HALF]
        body = jnp.where(slot == 0, rows[:BODY], rows[BODY + 2 * HALF :])
        last = jnp.where(slot == 0, shared, pltpu.roll(shared, HALF, 0))[:HALF]
        block = jnp.concatenate([body, last], axis=0)
        out_ref[:, i * NB : (i + 1) * NB] = block.astype(jnp.bfloat16)


def true_kernel(lat_ref, spec_weight_ref, target_ref, true_ref, energy_ref):
    true = jnp.zeros((CP, 2 * K), jnp.float32)
    for a in range(LAT_DEV):
        g = target_ref[a * CP : (a + 1) * CP, :].astype(jnp.float32)
        true = true + lat_ref[a] * g * g
    true = true[:, :K] + true[:, K:]
    true_ref[...] = true
    energy = jnp.sum(true * spec_weight_ref[...], axis=(0, 1), keepdims=True)
    energy_ref[...] = jnp.broadcast_to(energy, energy_ref.shape)


def middle_kernel(scale, parts_ref, spec_weight_ref, out_ref):
    sums = jnp.sum(parts_ref[...], axis=0)
    pred_power, true_power, cross_sum = sums[:, :K], sums[:, K : 2 * K], sums[:, 2 * K : 3 * K]
    energy = sums[:, 3 * K : 3 * K + 1] * scale + epsilon
    loss_scale = spec_weight_ref[...] / energy
    amp_pred = jnp.sqrt(pred_power + epsilon)
    amp_true = jnp.sqrt(true_power + epsilon)
    d_pred = (
        loss_scale
        * (
            4.0 * amp_pred
            - 2.0 * amp_true
            - cross_sum * (1.0 / amp_true - amp_true / (amp_pred * amp_pred))
        )
        / (2.0 * amp_pred)
    )
    d_cross = -loss_scale * (amp_pred / amp_true + amp_true / amp_pred)
    both = jnp.concatenate([d_pred, d_cross], axis=1)
    out_ref[...] = jnp.broadcast_to(both[None], out_ref.shape)


def one_hot(ref_row):
    owner = ref_row >> 8
    place = ref_row & (LO - 1)
    rows = lax.broadcasted_iota(jnp.int32, (LO, ref_row.shape[1]), 0)
    return owner, (rows == place).astype(jnp.float32).astype(jnp.bfloat16)


def shared_owner(owner):
    first = lax.broadcasted_iota(jnp.int32, (2 * HALF, owner.shape[1]), 0) < HALF
    wanted = jnp.where(first, 0, 1)
    return jnp.where((owner & 1) == wanted, owner >> 1, -1)


def forward_kernel(owners, lat_ref, buf_ref, cell_ref, weight_ref, table_ref, target_ref,
                   true_ref, *refs):
    energy_refs = refs[:-6]
    spec_ref, sums_ref, staged, nodes, grid, half_rows = refs[-6:]
    first = first_rows(NB)
    for p in range(owners // 2):
        even = buf_ref[2 * p].astype(jnp.float32)
        odd = buf_ref[2 * p + 1].astype(jnp.float32)
        middle = slice(BODY, BODY + 2 * HALF)
        tail = slice(BODY + 2 * HALF, PAIR)
        at = p * PAIR
        staged[at : at + BODY, :NB], staged[at : at + BODY, NB:] = even[:BODY], even[tail]
        staged[at + BODY : at + BODY + 2 * HALF, :NB] = jnp.where(
            first, even[middle], pltpu.roll(odd[middle], HALF, 0)
        )
        staged[at + BODY : at + BODY + 2 * HALF, NB:] = jnp.where(
            first, pltpu.roll(even[middle], HALF, 0), odd[middle]
        )
        staged[at + BODY + 2 * HALF : at + PAIR, :NB] = odd[:BODY]
        staged[at + BODY + 2 * HALF : at + PAIR, NB:] = odd[tail]
    nodes[...] = staged[...].astype(jnp.bfloat16)

    def row(a, _):
        for t in range(MAIN // TILE):
            cols = slice(t * TILE, (t + 1) * TILE)
            total = jnp.zeros((CP, TILE), jnp.float32)
            for m in range(J):
                owner, hot = one_hot(cell_ref[m, pl.ds(a, 1), cols])
                shared = shared_owner(owner)
                picked = jnp.dot(nodes[...], hot, preferred_element_type=jnp.float32)
                body = jnp.zeros((BODY, TILE), jnp.float32)
                half = jnp.zeros((2 * HALF, TILE), jnp.float32)
                for p in range(owners // 2):
                    block = picked[p * PAIR : (p + 1) * PAIR]
                    body = jnp.where(owner == 2 * p, block[:BODY], body)
                    half = jnp.where(shared == p, block[BODY : BODY + 2 * HALF], half)
                    body = jnp.where(owner == 2 * p + 1, block[BODY + 2 * HALF :], body)
                value = jnp.concatenate([body, half + pltpu.roll(half, HALF, 0)], axis=0)
                total = total + weight_ref[m, pl.ds(a, 1), cols] * value
            grid[pl.ds(pl.multiple_of(a * CP, CP), CP), cols] = total.astype(jnp.bfloat16)
        return 0

    lax.fori_loop(0, CELL_ROWS, row, 0, unroll=3)
    rest = grid[ROWS : ROWS + CP, :].astype(jnp.float32)
    zeros = jnp.zeros((CP, HALF_PAD - HALF_LON), jnp.float32)
    for a in range(LAT_DEV):
        for h in range(2):
            at = a * REST + h * HALF_REST
            piece = jnp.concatenate([rest[:, at : at + HALF_REST], zeros], axis=1)
            rows = slice(h * ROWS + a * CP, h * ROWS + (a + 1) * CP)
            half_rows[rows, HALF_MAIN:] = piece.astype(jnp.bfloat16)
    for h in range(2):
        columns = slice(h * HALF_MAIN, (h + 1) * HALF_MAIN)
        half_rows[h * ROWS : (h + 1) * ROWS, :HALF_MAIN] = grid[:ROWS, columns]
    halves = lax.dot_general(
        half_rows[...], table_ref[...], (((1,), (1,)), ((), ())),
        preferred_element_type=jnp.float32,
    )
    spectrum = halves[:ROWS] + half_sign() * halves[ROWS:]
    spec_ref[...] = spectrum.astype(jnp.bfloat16)
    pred = jnp.zeros((CP, 2 * K), jnp.float32)
    cross = jnp.zeros((CP, 2 * K), jnp.float32)
    for a in range(LAT_DEV):
        s = spec_ref[a * CP : (a + 1) * CP, :].astype(jnp.float32)
        g = target_ref[a * CP : (a + 1) * CP, :].astype(jnp.float32)
        ws = lat_ref[a] * s
        pred = pred + ws * s
        cross = cross + ws * g
    sums_ref[:, 0, :K] = pred[:, :K] + pred[:, K:]
    sums_ref[:, 0, K : 2 * K] = true_ref[...]
    sums_ref[:, 0, 2 * K : 3 * K] = cross[:, :K] + cross[:, K:]
    energy = sum((ref[0:1, :] for ref in energy_refs[1:]), energy_refs[0][0:1, :])
    sums_ref[:, 0, 3 * K :] = jnp.broadcast_to(energy, (CP, NB))


def backward_kernel(owners, lat_ref, cell_ref, weight_ref, table_ref, target_ref, spec_ref,
                    factor_ref, out_ref, grads, total, gated):
    d_pred, d_cross = factor_ref[:, 0, :K], factor_ref[:, 0, K:]
    sign = half_sign()[:, :K]
    for a in range(LAT_DEV):
        rows = slice(a * CP, (a + 1) * CP)
        for r in range(2):
            cols = slice(r * K, (r + 1) * K)
            s = spec_ref[rows, cols].astype(jnp.float32)
            g = target_ref[rows, cols].astype(jnp.float32)
            grad = lat_ref[a] * (2.0 * s * d_pred + g * d_cross)
            grads[rows, cols] = grad.astype(jnp.bfloat16)
            flipped = slice(ROWS + a * CP, ROWS + (a + 1) * CP)
            grads[flipped, cols] = (grad * sign).astype(jnp.bfloat16)
    grid_grad = jnp.dot(grads[...], table_ref[...], preferred_element_type=jnp.float32)
    rest = []
    for h in range(2):
        columns = slice(h * HALF_MAIN, (h + 1) * HALF_MAIN)
        gated[:ROWS, columns] = grid_grad[h * ROWS : (h + 1) * ROWS, :HALF_MAIN]
    for a in range(LAT_DEV):
        for h in range(2):
            rows = slice(h * ROWS + a * CP, h * ROWS + (a + 1) * CP)
            rest.append(grid_grad[rows, HALF_MAIN:HALF_LON])
    gated[ROWS:, :] = jnp.concatenate(rest, axis=1)
    total[...] = jnp.zeros_like(total)

    def row(a, _):
        for t in range(MAIN // TILE):
            cols = slice(t * TILE, (t + 1) * TILE)
            value = gated[pl.ds(pl.multiple_of(a * CP, CP), CP), cols]
            for m in range(J):
                owner, hot = one_hot(cell_ref[m, pl.ds(a, 1), cols])
                shared = shared_owner(owner)
                part = weight_ref[m, pl.ds(a, 1), cols] * value
                body, last = part[:BODY], part[BODY:]
                first = lax.broadcasted_iota(jnp.int32, last.shape, 0) < HALF
                half = jnp.where(first, last, pltpu.roll(last, HALF, 0))
                pieces = []
                for p in range(owners // 2):
                    pieces.append(jnp.where(owner == 2 * p, body, 0.0))
                    pieces.append(jnp.where(shared == p, half, 0.0))
                    pieces.append(jnp.where(owner == 2 * p + 1, body, 0.0))
                spread = jnp.concatenate(pieces, axis=0).astype(jnp.bfloat16)
                total[...] += lax.dot_general(
                    spread, hot, (((1,), (1,)), ((), ())), preferred_element_type=jnp.float32
                )
        return 0

    lax.fori_loop(0, CELL_ROWS, row, 0, unroll=3)
    first = first_rows(NB)
    for p in range(owners // 2):
        block = total[p * PAIR : (p + 1) * PAIR, :]
        left, right = block[BODY : BODY + 2 * HALF, :NB], block[BODY : BODY + 2 * HALF, NB:]
        even = jnp.where(first, left, pltpu.roll(right, HALF, 0))
        odd = jnp.where(first, pltpu.roll(left, HALF, 0), right)
        body = block[:BODY]
        out_ref[2 * p] = jnp.concatenate([body[:, :NB], even, body[:, NB:]], axis=0).astype(
            jnp.bfloat16
        )
        body = block[BODY + 2 * HALF :]
        out_ref[2 * p + 1] = jnp.concatenate([body[:, :NB], odd, body[:, NB:]], axis=0).astype(
            jnp.bfloat16
        )


SMEM = pl.BlockSpec(memory_space=pltpu.SMEM)
VMEM = pl.BlockSpec(memory_space=pltpu.VMEM)
PARAMS = pltpu.CompilerParams(vmem_limit_bytes=24 * 1024 * 1024)


def exchange(blocks, axis):
    return lax.all_to_all(blocks, axis, split_axis=0, concat_axis=0, tiled=True)


def everyone(block, axis):
    count = lax.axis_size(axis)
    block = block + lax.ppermute(block, axis, [(i, i ^ 1) for i in range(count)])
    shifts = [[(i, (i + d) % count) for i in range(count)] for d in range(2, count, 2)]
    return [block] + [lax.ppermute(block, axis, shift) for shift in shifts]


def cell_rows(cells):
    first, second = cells[:, :, :HALF_LON], cells[:, :, HALF_LON:]
    rest = jnp.concatenate([first[:, :, HALF_MAIN:], second[:, :, HALF_MAIN:]], axis=2)
    main = jnp.concatenate([first[:, :, :HALF_MAIN], second[:, :, :HALF_MAIN]], axis=2)
    return jnp.concatenate([main, rest.reshape(J, 1, LAT_DEV * REST)], axis=1)


def shards(node_values, block_slot, cell_ref, cell_weight, target_spectrum, spec_weight):
    owners = lax.axis_size("band")
    band_index = lax.axis_index("band")
    samples, chans, nodes_local = node_values.shape
    lat_total = LAT_DEV * owners
    lat_weight = lat_weights(band_index * LAT_DEV, LAT_DEV, lat_total)
    table = jnp.asarray(dft_table())

    outgoing = pl.pallas_call(
        pack_kernel,
        out_shape=jax.ShapeDtypeStruct((owners, PAIR, NB), jnp.bfloat16),
        in_specs=[SMEM, VMEM],
        out_specs=VMEM,
        scratch_shapes=[pltpu.VMEM((owners, PAIR, NB), jnp.float32)],
        compiler_params=pltpu.CompilerParams(vmem_limit_bytes=60 * 1024 * 1024),
        name="pack",
    )(block_slot, node_values[0])
    outgoing, target_spectrum, cell_ref, cell_weight, spec_weight = lax.optimization_barrier(
        (outgoing, target_spectrum, cell_ref, cell_weight, spec_weight)
    )
    received = exchange(outgoing, "band")

    refs = cell_rows(cell_ref)
    weights = cell_rows(cell_weight)
    target = jnp.pad(
        jnp.transpose(target_spectrum[0].reshape(chans, LAT_DEV, 2 * K), (1, 0, 2)),
        ((0, 0), (0, CP - chans), (0, 0)),
    ).reshape(ROWS, 2 * K)

    true_part, energy_part = pl.pallas_call(
        true_kernel,
        out_shape=(
            jax.ShapeDtypeStruct((CP, K), jnp.float32),
            jax.ShapeDtypeStruct((8, 128), jnp.float32),
        ),
        in_specs=[SMEM, VMEM, VMEM],
        out_specs=(VMEM, VMEM),
        compiler_params=PARAMS,
        name="true_power",
    )(lat_weight, spec_weight[None, :], target)
    energies = everyone(energy_part, "chan")

    spectrum, sums = pl.pallas_call(
        functools.partial(forward_kernel, owners),
        out_shape=(
            jax.ShapeDtypeStruct((ROWS, 2 * K), jnp.bfloat16),
            jax.ShapeDtypeStruct((CP, 1, 3 * K + NB), jnp.float32),
        ),
        in_specs=[SMEM] + [VMEM] * (6 + len(energies)),
        out_specs=(VMEM, VMEM),
        scratch_shapes=[
            pltpu.VMEM((owners * CHANS, LO), jnp.float32),
            pltpu.VMEM((owners * CHANS, LO), jnp.bfloat16),
            pltpu.VMEM((CELL_ROWS * CP, MAIN), jnp.bfloat16),
            pltpu.VMEM((2 * ROWS, HALF_PAD), jnp.bfloat16),
        ],
        compiler_params=PARAMS,
        name="forward",
    )(lat_weight, received, refs, weights, table, target, true_part, *energies)

    parts = exchange(sums, "band")
    factors = pl.pallas_call(
        functools.partial(middle_kernel, 1.0 / (C * K * lat_total)),
        out_shape=jax.ShapeDtypeStruct((owners, 1, 2 * K), jnp.float32),
        in_specs=[VMEM, VMEM],
        out_specs=VMEM,
        compiler_params=PARAMS,
        name="middle",
    )(parts, spec_weight[None, :])
    factors = exchange(factors, "band")

    slot_grad = pl.pallas_call(
        functools.partial(backward_kernel, owners),
        out_shape=jax.ShapeDtypeStruct((owners, PAIR, NB), jnp.bfloat16),
        in_specs=[SMEM] + [VMEM] * 6,
        out_specs=VMEM,
        scratch_shapes=[
            pltpu.VMEM((2 * ROWS, 2 * K), jnp.bfloat16),
            pltpu.VMEM((owners * CHANS, LO), jnp.float32),
            pltpu.VMEM((CELL_ROWS * CP, MAIN), jnp.float32),
        ],
        compiler_params=PARAMS,
        name="backward",
    )(lat_weight, refs, weights, table, target, spectrum, factors)

    returned = exchange(slot_grad, "band")
    node_grad = pl.pallas_call(
        unpack_kernel,
        out_shape=jax.ShapeDtypeStruct((chans, nodes_local), jnp.bfloat16),
        in_specs=[SMEM, VMEM],
        out_specs=VMEM,
        compiler_params=PARAMS,
        name="unpack",
    )(block_slot, returned)
    return node_grad[None]


def solution(mesh):
    in_specs = (
        P(None, "chan", "band"),
        P("band"),
        P(None, "band", None),
        P(None, "band", None),
        P(None, "chan", "band", None, None),
        P(),
    )
    out_specs = P(None, "chan", "band")
    return jax.shard_map(shards, mesh=mesh, in_specs=in_specs, out_specs=out_specs, check_vma=False)
```
